32 devices in a mesh: row: 8 (over z, y), col: 4 (over x, core).
Axes of the slice: x: 2, y: 2, z: 4, core: 2. Of those that a mesh axis runs over, the one named last changes fastest.
Arguments:
- panel_one: bfloat16 [512, 8192], P('col', 'row'), may hold values from -1.1953125 to 1.1953125
- panel_two: bfloat16 [512, 8192], P('col', 'row'), may hold values from -3 to 3
- inverse_one: bfloat16 [512, 512], replicated
- inverse_two: bfloat16 [512, 512], replicated
- column_blocks: int32 [4], replicated, may hold values from 0 to 63, as said below
- row_map: int32 [64], P('row'), may hold values from 0 to 63, as said below
- targets: bfloat16 [8, 4, 128, 128, 128], P('row', 'col'), may hold values from -6 to 6
- rows_one: int32 [8, 4, 128], P('row', 'col'), may hold values from 0 to 63, as said below
- cols_one: int32 [8, 4, 128], P('row', 'col'), may hold values from 0 to 63, as said below
- rows_two: int32 [8, 4, 128], P('row', 'col'), may hold values from 0 to 63, as said below
- cols_two: int32 [8, 4, 128], P('row', 'col'), may hold values from 0 to 63, as said below
Outputs:
- lower_one: bfloat16 [512, 8192], P('col', 'row')
- lower_two: bfloat16 [512, 8192], P('col', 'row')
- trailing: bfloat16 [8, 4, 128, 128, 128], P('row', 'col')
The draws below stay inside these ranges and needn't reach their ends.
Inputs may be any that keep to these rules, and one draw needn't show every extreme that they name: `column_blocks`: the entries are distinct. row_map[j] // 8 equals j // 8; within each aligned run of 8 entries every value of the run appears once. rows_one[r, c, s] // 8 equals r. cols_one[r, c, s] % 4 equals c. rows_two[r, c, s] // 8 equals r. cols_two[r, c, s] % 4 equals c.
All inputs are finite; a program needn't handle non-finite values.
Results may differ from the reference program's by a relative error of at most 0.006.
Values may be sent and summed in bfloat16 or wider, within the bound.
No kernel may reach another device: no remote copies, remote signals or barrier semaphores. Data moves between devices by JAX's collectives and lax.ppermute only.
A program may use at most 192 MiB of HBM per device.

```python
import math
import jax
import jax.numpy as jnp
from jax import lax

W = 512
B = 128
RB_DEV = 8
TB_DEV = 128
GR = 8
GC = 4
ROWBLOCKS = 64
ROWS = 8192
NCB = 4


def triangle(key, diag_low, diag_high, off_scale):
    key_diag, key_off = jax.random.split(key)
    positions = jnp.arange(W)
    lower_mask = positions[:, None] > positions[None, :]
    diagonal = jax.random.uniform(key_diag, (W,), jnp.float32, diag_low, diag_high)
    spread = jax.random.normal(key_off, (W, W), jnp.float32) * (off_scale / math.sqrt(W))
    matrix = jnp.where(lower_mask, spread, 0.0) + jnp.diag(diagonal)
    return matrix.astype(jnp.bfloat16)


def draw_inverse_one(key, part):
    return triangle(jax.random.fold_in(key, 11), 0.6, 1.0, 0.4)


def draw_inverse_two(key, part):
    return triangle(jax.random.fold_in(key, 12), 0.15, 0.3, 0.08)


def draw_column_blocks(key, part):
    return jax.random.permutation(key, ROWBLOCKS)[:NCB].astype(jnp.int32)


def draw_row_map(key, part):
    scores = jax.random.randint(key, (GR, RB_DEV), 0, 1 << 20, dtype=jnp.int32) * RB_DEV
    scores = scores + jnp.arange(RB_DEV, dtype=jnp.int32)[None, :]
    order = jnp.argsort(scores, axis=1, stable=True).astype(jnp.int32)
    base_rows = jnp.arange(GR, dtype=jnp.int32)[:, None] * RB_DEV
    return (base_rows + order).reshape(ROWBLOCKS).astype(jnp.int32)


def owner_rows(key):
    grid_rows = jnp.arange(GR, dtype=jnp.int32).reshape(GR, 1, 1)
    offsets = jax.random.randint(key, (GR, GC, TB_DEV), 0, RB_DEV, dtype=jnp.int32)
    return (grid_rows * RB_DEV + offsets).astype(jnp.int32)


def owner_cols(key):
    grid_cols = jnp.arange(GC, dtype=jnp.int32).reshape(1, GC, 1)
    strides = jax.random.randint(key, (GR, GC, TB_DEV), 0, ROWBLOCKS // GC, dtype=jnp.int32)
    return (grid_cols + GC * strides).astype(jnp.int32)


def draw_rows_one(key, part):
    return owner_rows(jax.random.fold_in(key, 21))


def draw_cols_one(key, part):
    return owner_cols(jax.random.fold_in(key, 22))


def draw_rows_two(key, part):
    return owner_rows(jax.random.fold_in(key, 23))


def draw_cols_two(key, part):
    return owner_cols(jax.random.fold_in(key, 24))


def shard_levels(own_key, shape, cuts, smallest, high):
    def one(dim, shards_of):
        steps = jax.random.uniform(jax.random.fold_in(jax.random.fold_in(own_key, 6), dim), (shards_of,), jnp.float32, smallest / len(cuts), high / len(cuts))
        return jnp.repeat(jnp.exp(steps), shape[dim] // shards_of).reshape((-1,) + (1,) * (len(shape) - dim - 1))

    loudness = one(*cuts[0])
    for cut in cuts[1:]:
        loudness = loudness * one(*cut)
    return loudness


def normal_values(rng, extent, width, most, pieces=(), kind=jnp.bfloat16):
    entries = width * jax.random.normal(rng, extent, jnp.float32)
    if pieces:
        entries = entries * shard_levels(rng, extent, pieces, -0.22, 0.18)
    return jnp.clip(entries, -most, most).astype(kind)


def setup_inputs(seed: int = 0) -> dict:
    key_list = jax.random.split(jax.random.key(seed), 12)
    panel_one = normal_values(key_list[0], (W, ROWS), 0.2, 1.1953125, ((0, 4), (1, 8)))
    panel_two = normal_values(key_list[1], (W, ROWS), 0.5, 3.0, ((0, 4), (1, 8)))
    inverse_one = draw_inverse_one(jax.random.fold_in(key_list[11], 71), 0)
    inverse_two = draw_inverse_two(jax.random.fold_in(key_list[11], 71), 0)
    column_blocks = draw_column_blocks(jax.random.fold_in(key_list[11], 71), 0)
    row_map = draw_row_map(jax.random.fold_in(key_list[11], 71), 0)
    targets = normal_values(key_list[6], (GR, GC, TB_DEV, B, B), 1.0, 6.0, ((0, 8), (1, 4)))
    rows_one = draw_rows_one(jax.random.fold_in(key_list[11], 71), 0)
    cols_one = draw_cols_one(jax.random.fold_in(key_list[11], 71), 0)
    rows_two = draw_rows_two(jax.random.fold_in(key_list[11], 71), 0)
    cols_two = draw_cols_two(jax.random.fold_in(key_list[11], 71), 0)
    return dict(panel_one=panel_one, panel_two=panel_two, inverse_one=inverse_one, inverse_two=inverse_two, column_blocks=column_blocks, row_map=row_map, targets=targets, rows_one=rows_one, cols_one=cols_one, rows_two=rows_two, cols_two=cols_two)


def reference(panel_one, panel_two, inverse_one, inverse_two, column_blocks, row_map, targets, rows_one, cols_one, rows_two, cols_two):
    lower_one = jnp.dot(inverse_one, panel_one, preferred_element_type=jnp.float32).astype(jnp.bfloat16)
    blocks_one = lower_one.reshape(W, ROWBLOCKS, B)
    bridge = jnp.take(blocks_one, column_blocks.astype(jnp.int32), axis=1).reshape(W, W)
    mapped = jnp.take(blocks_one, row_map.astype(jnp.int32), axis=1).reshape(W, ROWS)
    update = jnp.dot(bridge.T, mapped, preferred_element_type=jnp.float32)
    updated = (panel_two.astype(jnp.float32) - update).astype(jnp.bfloat16)
    lower_two = jnp.dot(inverse_two, updated, preferred_element_type=jnp.float32).astype(jnp.bfloat16)
    blocks_two = lower_two.reshape(W, ROWBLOCKS, B)

    def slot_update(slot_pack):
        first_rows, first_cols, second_rows, second_cols, old_blocks = slot_pack
        left_one = jnp.take(blocks_one, first_rows, axis=1).astype(jnp.float32)
        right_one = jnp.take(blocks_one, first_cols, axis=1).astype(jnp.float32)
        left_two = jnp.take(blocks_two, second_rows, axis=1).astype(jnp.float32)
        right_two = jnp.take(blocks_two, second_cols, axis=1).astype(jnp.float32)
        term_one = jnp.einsum("wsx,wsy->sxy", left_one, right_one)
        term_two = jnp.einsum("wsx,wsy->sxy", left_two, right_two)
        return (old_blocks.astype(jnp.float32) - term_one - term_two).astype(jnp.bfloat16)

    grid_count = GR * GC
    trailing = lax.map(slot_update, (rows_one.reshape(grid_count, TB_DEV).astype(jnp.int32),
                                      cols_one.reshape(grid_count, TB_DEV).astype(jnp.int32),
                                      rows_two.reshape(grid_count, TB_DEV).astype(jnp.int32),
                                      cols_two.reshape(grid_count, TB_DEV).astype(jnp.int32),
                                      targets.reshape(grid_count, TB_DEV, B, B)))
    return lower_one, lower_two, trailing.reshape(GR, GC, TB_DEV, B, B)
```

```python
import functools

import jax
import jax.numpy as jnp
from jax import lax
from jax.experimental import pallas as pl
from jax.experimental.pallas import tpu as pltpu
from jax.sharding import PartitionSpec as P

VMEM = pl.BlockSpec(memory_space=pltpu.VMEM)
SMEM = pl.BlockSpec(memory_space=pltpu.SMEM)
F32 = jnp.float32
BF16 = jnp.bfloat16
TN = (((0,), (0,)), ((), ()))


def params(mib):
    return pltpu.CompilerParams(vmem_limit_bytes=mib << 20)


def xor_permute(value, axis, mask):
    return lax.ppermute(value, axis, [(i, i ^ mask) for i in range(lax.axis_size(axis))])


def xor_gather(value, axis):
    pieces = {0: value}
    bit = lax.axis_size(axis) // 2
    while bit:
        for m in list(pieces):
            pieces[m | bit] = xor_permute(pieces[m], axis, bit)
        bit //= 2
    return [pieces[m] for m in range(len(pieces))]


def xor_sum(value, axis):
    bit = 1
    while bit < lax.axis_size(axis):
        value = value + xor_permute(value, axis, bit)
        bit *= 2
    return value


def ring_order(count):
    return list(range(0, count, 2)) + list(range(count - 1, 0, -2))


def ring_gather(tile):
    count = lax.axis_size("row")
    order = ring_order(count)
    ahead = [(order[i], order[(i + 1) % count]) for i in range(count)]
    back = [(b, a) for a, b in ahead]
    forward, backward = [], []
    f = b = tile
    for _ in range(count // 2 - 1):
        f = lax.ppermute(f, "row", ahead)
        b = lax.ppermute(b, "row", back)
        forward.append(f)
        backward.append(b)
    half = tile.shape[0] // 2
    top = lax.ppermute(f[:half], "row", ahead)
    bottom = lax.ppermute(b[half:], "row", back)
    return [tile] + forward + [top, bottom] + backward[::-1]


def ring_distance(row):
    count = lax.axis_size("row")
    position = lambda r: jnp.where(r % 2 == 0, r // 2, count - 1 - r // 2)
    return (position(lax.axis_index("row")) - position(row)) % count


def bridge_kernel(block, local, blocks_ref, panel_ref, out_ref):
    row = lax.axis_index("row")
    for k in range(blocks_ref.shape[0]):
        chosen = blocks_ref[k]
        start = pl.multiple_of(chosen % local * block, block)
        piece = panel_ref[:, pl.ds(start, block)]
        keep = jnp.where(chosen // local == row, 1.0, 0.0).astype(BF16)
        out_ref[:, k * block : (k + 1) * block] = piece * keep


def bridge_columns(panel, column_blocks, block):
    slab = panel.shape[0]
    count = column_blocks.shape[0]
    return pl.pallas_call(
        functools.partial(bridge_kernel, block, panel.shape[1] // block),
        out_shape=jax.ShapeDtypeStruct((slab, count * block), BF16),
        in_specs=[SMEM, VMEM],
        out_specs=VMEM,
        name="bridge_columns",
    )(column_blocks, panel)


def assemble(pieces, full_ref):
    col = lax.axis_index("col")
    slab = pieces[0].shape[0]
    for m, piece in enumerate(pieces):
        start = pl.multiple_of((col ^ m) * slab, slab)
        full_ref[pl.ds(start, slab), :] = piece[...]


def store_parts(block, lower_ref, own_ref, tile_ref):
    col = lax.axis_index("col")
    slab = own_ref.shape[0]
    own_ref[...] = lower_ref[pl.ds(pl.multiple_of(col * slab, slab), slab), :]
    for t in range(tile_ref.shape[1] // block):
        start = pl.multiple_of((t * lax.axis_size("col") + col) * block, block)
        tile_ref[:, t * block : (t + 1) * block] = lower_ref[:, pl.ds(start, block)]


def multiply(left, right_ref, out_ref, step=256):
    for n in range(0, right_ref.shape[1], step):
        out_ref[:, n : n + step] = jnp.dot(
            left, right_ref[:, n : n + step], preferred_element_type=F32
        ).astype(out_ref.dtype)


def lower_one_kernel(block, *refs):
    inverse_ref, *pieces, lower_ref, own_ref, tile_ref, full_ref = refs
    assemble(pieces, full_ref)
    multiply(inverse_ref[...], full_ref, lower_ref)
    store_parts(block, lower_ref, own_ref, tile_ref)


def lower_shapes(width, slab, columns, block, cols):
    tiles = columns // block // cols
    return (
        jax.ShapeDtypeStruct((width, columns), BF16),
        jax.ShapeDtypeStruct((slab, columns), BF16),
        jax.ShapeDtypeStruct((width, tiles * block), BF16),
    )


def factor_one(inverse, pieces, block):
    width = inverse.shape[0]
    slab, columns = pieces[0].shape
    return pl.pallas_call(
        functools.partial(lower_one_kernel, block),
        out_shape=lower_shapes(width, slab, columns, block, len(pieces)),
        in_specs=[VMEM] * (1 + len(pieces)),
        out_specs=(VMEM,) * 3,
        scratch_shapes=[pltpu.VMEM((width, columns), BF16)],
        compiler_params=params(24),
        name="factor_one",
    )(inverse, *pieces)


def lower_two_kernel(block, count, *refs):
    map_ref, one_ref, two_ref, lower_one_ref = refs[:4]
    raw = refs[4 : 4 + count]
    pieces = refs[4 + count : 4 + 2 * count]
    lower_ref, own_ref, tile_ref, raw_ref, bridge_ref, mapped_ref, full_ref = refs[4 + 2 * count :]
    local = map_ref.shape[0]
    assemble(raw, raw_ref)
    assemble(pieces, full_ref)
    multiply(one_ref[...], raw_ref, bridge_ref)
    for j in range(local):
        start = pl.multiple_of(map_ref[j] % local * block, block)
        mapped_ref[:, j * block : (j + 1) * block] = lower_one_ref[:, pl.ds(start, block)]
    step = 256
    for n in range(0, full_ref.shape[1], step):
        update = lax.dot_general(
            bridge_ref[...], mapped_ref[:, n : n + step], TN, preferred_element_type=F32
        )
        mapped_ref[:, n : n + step] = (full_ref[:, n : n + step].astype(F32) - update).astype(BF16)
    multiply(two_ref[...], mapped_ref, lower_ref)
    store_parts(block, lower_ref, own_ref, tile_ref)


def factor_two(row_map, inverse_one, inverse_two, lower_one, raw, pieces, block):
    width = inverse_one.shape[0]
    slab, columns = pieces[0].shape
    count = len(pieces)
    return pl.pallas_call(
        functools.partial(lower_two_kernel, block, count),
        out_shape=lower_shapes(width, slab, columns, block, count),
        in_specs=[SMEM] + [VMEM] * (3 + 2 * count),
        out_specs=(VMEM,) * 3,
        scratch_shapes=[
            pltpu.VMEM((width, raw[0].shape[1]), BF16),
            pltpu.VMEM((width, raw[0].shape[1]), BF16),
            pltpu.VMEM((width, columns), BF16),
            pltpu.VMEM((width, columns), BF16),
        ],
        compiler_params=params(24),
        name="factor_two",
    )(row_map, inverse_one, inverse_two, lower_one, *raw, *pieces)


def transpose_kernel(block, in_ref, out_ref):
    for n in range(0, in_ref.shape[1], block):
        out_ref[n : n + block, :] = in_ref[:, n : n + block].T


def transposed(lower, block):
    return pl.pallas_call(
        functools.partial(transpose_kernel, block),
        out_shape=jax.ShapeDtypeStruct(lower.shape[::-1], BF16),
        in_specs=[VMEM],
        out_specs=VMEM,
        name="transposed",
    )(lower)


def schur_kernel(block, count, per_step, index_ref, left_ref, *refs):
    tiles = refs[: count + 1]
    base_ref, out_ref, products_ref = refs[count + 1 :]
    local = left_ref.shape[0] // block
    each = tiles[0].shape[1] // block
    half = left_ref.shape[1] // 2

    def store(distance, product):
        for t in range(each):
            for a in range(local):
                products_ref[(distance * each + t) * local + a] = product[
                    a * block : (a + 1) * block, t * block : (t + 1) * block
                ]

    @pl.when(pl.program_id(0) == 0)
    def _():
        for distance in range(count):
            if distance == count // 2:
                product = jnp.dot(
                    left_ref[:, :half], tiles[distance][...], preferred_element_type=F32
                )
                product = product + jnp.dot(
                    left_ref[:, half:], tiles[distance + 1][...], preferred_element_type=F32
                )
            else:
                tile = tiles[distance + (distance > count // 2)]
                product = jnp.dot(left_ref[...], tile[...], preferred_element_type=F32)
            store(distance, product)

    first = pl.program_id(0) * per_step
    for s in range(per_step):
        term = products_ref[index_ref[first + s]]
        out_ref[s] = (base_ref[s].astype(F32) - term).astype(out_ref.dtype)


def schur(index, left, tiles, base, dtype, per_step=16):
    slots, block, _ = base.shape
    count = len(tiles) - 1
    local = left.shape[0] // block
    each = tiles[0].shape[1] // block
    whole = lambda a: pl.BlockSpec(a.shape, lambda i, idx: (0, 0), pipeline_mode=pl.Buffered(1))
    moving = pl.BlockSpec((per_step, block, block), lambda i, idx: (i, 0, 0))
    return pl.pallas_call(
        functools.partial(schur_kernel, block, count, per_step),
        out_shape=jax.ShapeDtypeStruct(base.shape, dtype),
        grid_spec=pltpu.PrefetchScalarGridSpec(
            num_scalar_prefetch=1,
            grid=(slots // per_step,),
            in_specs=[whole(left)] + [whole(t) for t in tiles] + [moving],
            out_specs=moving,
            scratch_shapes=[pltpu.VMEM((count * each * local, block, block), F32)],
        ),
        compiler_params=params(40),
        name="schur",
    )(index, left, *tiles, base)


def slot_index(rows, cols, local):
    rows, cols = rows.reshape(-1), cols.reshape(-1)
    parts = lax.axis_size("col")
    tile = cols % local // parts
    return (ring_distance(cols // local) * (local // parts) + tile) * local + rows % local


def per_device(
    panel_one,
    panel_two,
    inverse_one,
    inverse_two,
    column_blocks,
    row_map,
    targets,
    rows_one,
    cols_one,
    rows_two,
    cols_two,
):
    block = targets.shape[-1]
    local = panel_one.shape[1] // block
    raw = xor_sum(bridge_columns(panel_one, column_blocks, block), "row")
    pieces_one = xor_gather(panel_one, "col")
    pieces_two = xor_gather(panel_two, "col")
    lower_one, own_one, tile_one = factor_one(inverse_one, pieces_one, block)
    tiles_one = ring_gather(tile_one)
    raw = xor_gather(raw, "col")
    lower_two, own_two, tile_two = factor_two(
        row_map, inverse_one, inverse_two, lower_one, raw, pieces_two, block
    )
    tiles_two = ring_gather(tile_two)
    base = targets.reshape(-1, block, block)
    part = schur(
        slot_index(rows_one, cols_one, local), transposed(lower_one, block), tiles_one, base, F32
    )
    trailing = schur(
        slot_index(rows_two, cols_two, local), transposed(lower_two, block), tiles_two, part, BF16
    )
    return own_one, own_two, trailing.reshape(targets.shape)


def solution(mesh):
    return jax.shard_map(
        per_device,
        mesh=mesh,
        in_specs=(
            P("col", "row"),
            P("col", "row"),
            P(),
            P(),
            P(),
            P("row"),
            P("row", "col", None, None, None),
            P("row", "col", None),
            P("row", "col", None),
            P("row", "col", None),
            P("row", "col", None),
        ),
        out_specs=(P("col", "row"), P("col", "row"), P("row", "col", None, None, None)),
        check_vma=False,
    )
```

```python
import functools

import jax
import jax.numpy as jnp
from jax import lax
from jax.experimental import pallas as pl
from jax.experimental.pallas import tpu as pltpu
from jax.sharding import PartitionSpec as P

VMEM = pl.BlockSpec(memory_space=pltpu.VMEM)
SMEM = pl.BlockSpec(memory_space=pltpu.SMEM)
HBM = pl.BlockSpec(memory_space=pltpu.HBM)
ANY = pl.BlockSpec(memory_space=pl.ANY)
F32 = jnp.float32
BF16 = jnp.bfloat16
TN = (((0,), (0,)), ((), ()))


def call(kernel, name, mib, micros, **kwargs):
    return pl.pallas_call(
        kernel,
        compiler_params=pltpu.CompilerParams(vmem_limit_bytes=mib and mib << 20),
        cost_estimate=pl.CostEstimate(
            flops=0, bytes_accessed=int(micros * 1e6), transcendentals=0
        ),
        name=name,
        **kwargs,
    )


def after(value, *earlier):
    return lax.optimization_barrier((value,) + earlier)[0]


def xor_permute(value, axis, mask):
    return lax.ppermute(value, axis, [(i, i ^ mask) for i in range(lax.axis_size(axis))])


def far_pieces(value):
    pieces = {0: value}
    bit = lax.axis_size("col") // 2
    while bit > 1:
        for m in list(pieces):
            pieces[m | bit] = xor_permute(pieces[m], "col", bit)
        bit //= 2
    return pieces


def near_pieces(pieces):
    pieces = dict(pieces)
    for m in list(pieces):
        pieces[m ^ 1] = xor_permute(pieces[m], "col", 1)
    return [pieces[m] for m in range(len(pieces))]


def ring_order(count):
    return list(range(0, count, 2)) + list(range(count - 1, 0, -2))


def ring_step(forward, backward):
    count = lax.axis_size("row")
    order = ring_order(count)
    ahead = [(order[i], order[(i + 1) % count]) for i in range(count)]
    back = [(b, a) for a, b in ahead]
    return lax.ppermute(forward, "row", ahead), lax.ppermute(backward, "row", back)


def arrival_rank(row):
    count = lax.axis_size("row")
    position = lambda r: jnp.where(r % 2 == 0, r // 2, count - 1 - r // 2)
    distance = (position(lax.axis_index("row")) - position(row)) % count
    ahead = jnp.maximum(2 * distance - 1, 0)
    return jnp.where(distance <= count // 2, ahead, 2 * (count - distance))


def slot_products(rows, cols, local):
    each = local // lax.axis_size("col")
    tile = cols % local // lax.axis_size("col")
    return (arrival_rank(cols // local) * each + tile) * local + rows % local


def late_slots(products, first):
    slots = products.shape[0]
    places = jnp.arange(slots, dtype=jnp.int32)
    late = products >= first
    place = jnp.sum(late[None, :] & (places[None, :] < places[:, None]), -1, dtype=jnp.int32)
    code = products * slots + places
    here = late[None, :] & (place[None, :] == places[:, None])
    table = jnp.sum(jnp.where(here, code[None, :], 0), -1, dtype=jnp.int32)
    return table, jnp.sum(late, dtype=jnp.int32).reshape(1)


def staged(value):
    return value * lax.optimization_barrier(jnp.ones((), value.dtype))


def bridge_kernel(block, local, blocks_ref, panel_ref, out_ref):
    row = lax.axis_index("row")
    for k in range(blocks_ref.shape[0]):
        piece = panel_ref[:, column(blocks_ref[k] % local, block)]
        keep = jnp.where(blocks_ref[k] // local == row, 1.0, 0.0).astype(BF16)
        out_ref[:, k * block : (k + 1) * block] = piece * keep


def bridge_columns(panel, column_blocks, block):
    slab = panel.shape[0]
    count = column_blocks.shape[0]
    return call(
        functools.partial(bridge_kernel, block, panel.shape[1] // block),
        "bridge_columns",
        None,
        1.3,
        out_shape=jax.ShapeDtypeStruct((slab, count * block), BF16),
        in_specs=[SMEM, VMEM],
        out_specs=VMEM,
    )(column_blocks, panel)


def slab_place(m, slab):
    start = pl.multiple_of((lax.axis_index("col") ^ m) * slab, slab)
    return pl.ds(start, slab)


def transposed_dot(left, right):
    return lax.dot_general(left, right, TN, preferred_element_type=F32)


def multiply(left_ref, right_ref, out_ref, step=256):
    for n in range(0, right_ref.shape[1], step):
        out_ref[:, n : n + step] = jnp.dot(
            left_ref[...], right_ref[:, n : n + step], preferred_element_type=F32
        ).astype(out_ref.dtype)


def column(j, block):
    return pl.ds(pl.multiple_of(j * block, block), block)


def own_blocks(block, width):
    for t in range(width // block):
        j = t * lax.axis_size("col") + lax.axis_index("col")
        yield slice(t * block, (t + 1) * block), j


def factor_one_kernel(block, count, *refs):
    inverse_ref, *pieces = refs[: 1 + count]
    lower_ref, own_ref, tile_ref, full_ref = refs[1 + count :]
    slab = own_ref.shape[0]
    for m, piece in enumerate(pieces):
        full_ref[slab_place(m, slab), :] = piece[...]
    multiply(inverse_ref, full_ref, lower_ref)
    own_ref[...] = lower_ref[slab_place(0, slab), :]
    for part, j in own_blocks(block, tile_ref.shape[1]):
        tile_ref[:, part] = lower_ref[:, column(j, block)]


def factor_one(inverse, pieces, block):
    width = inverse.shape[0]
    slab, columns = pieces[0].shape
    count = len(pieces)
    return call(
        functools.partial(factor_one_kernel, block, count),
        "factor_one",
        12,
        1.6,
        out_shape=(
            jax.ShapeDtypeStruct((width, columns), BF16),
            jax.ShapeDtypeStruct((slab, columns), BF16),
            jax.ShapeDtypeStruct((width, columns // count), BF16),
        ),
        in_specs=[VMEM] * (1 + count),
        out_specs=(VMEM,) * 3,
        scratch_shapes=[pltpu.VMEM((width, columns), BF16)],
    )(inverse, *pieces)


def tile_two_kernel(block, count, *refs):
    map_ref, one_ref, two_ref, lower_one_ref = refs[:4]
    raw = refs[4 : 4 + count]
    pieces = refs[4 + count : 4 + 2 * count]
    tile_ref, bridge_ref, raw_ref, full_ref, mapped_ref = refs[4 + 2 * count :]
    slab = raw[0].shape[0]
    for m, piece in enumerate(raw):
        raw_ref[slab_place(m, slab), :] = piece[...]
    multiply(one_ref, raw_ref, bridge_ref)
    for part, j in own_blocks(block, tile_ref.shape[1]):
        for m, piece in enumerate(pieces):
            full_ref[slab_place(m, slab), part] = piece[:, column(j, block)]
        mapped_ref[:, part] = lower_one_ref[:, column(map_ref[j], block)]
    update = transposed_dot(bridge_ref[...], mapped_ref[...])
    mapped_ref[...] = (full_ref[...].astype(F32) - update).astype(BF16)
    multiply(two_ref, mapped_ref, tile_ref)


def tile_two(row_map, inverse_one, inverse_two, lower_one, raw, pieces, block):
    width = inverse_one.shape[0]
    columns = pieces[0].shape[1]
    count = len(pieces)
    tile = columns // count
    return call(
        functools.partial(tile_two_kernel, block, count),
        "tile_two",
        12,
        1.6,
        out_shape=(
            jax.ShapeDtypeStruct((width, tile), BF16),
            jax.ShapeDtypeStruct((width, raw[0].shape[1]), BF16),
        ),
        in_specs=[SMEM] + [VMEM] * (3 + 2 * count),
        out_specs=(VMEM,) * 2,
        scratch_shapes=[
            pltpu.VMEM((width, raw[0].shape[1]), BF16),
            pltpu.VMEM((width, tile), BF16),
            pltpu.VMEM((width, tile), BF16),
        ],
    )(row_map, inverse_one, inverse_two, lower_one, *raw, *pieces)


def factor_two_kernel(block, count, *refs):
    map_ref, two_ref, lower_one_ref, bridge_ref, *pieces = refs[: 4 + count]
    lower_ref, own_ref, full_ref, mapped_ref = refs[4 + count :]
    slab = own_ref.shape[0]
    for m, piece in enumerate(pieces):
        full_ref[slab_place(m, slab), :] = piece[...]
    for j in range(map_ref.shape[0]):
        mapped_ref[:, j * block : (j + 1) * block] = lower_one_ref[:, column(map_ref[j], block)]
    step = 256
    for n in range(0, full_ref.shape[1], step):
        part = slice(n, n + step)
        update = transposed_dot(bridge_ref[...], mapped_ref[:, part])
        mapped_ref[:, part] = (full_ref[:, part].astype(F32) - update).astype(BF16)
    multiply(two_ref, mapped_ref, lower_ref)
    own_ref[...] = lower_ref[slab_place(0, slab), :]


def factor_two(row_map, inverse_two, lower_one, bridge, pieces, block):
    width = inverse_two.shape[0]
    slab, columns = pieces[0].shape
    count = len(pieces)
    return call(
        functools.partial(factor_two_kernel, block, count),
        "factor_two",
        12,
        2.4,
        out_shape=(
            jax.ShapeDtypeStruct((width, columns), BF16),
            jax.ShapeDtypeStruct((slab, columns), BF16),
        ),
        in_specs=[SMEM] + [VMEM] * (3 + count),
        out_specs=(VMEM,) * 2,
        scratch_shapes=[pltpu.VMEM((width, columns), BF16), pltpu.VMEM((width, columns), BF16)],
    )(row_map, inverse_two, lower_one, bridge, *pieces)


def products_of(left_ref, tiles, products_ref, block):
    local = left_ref.shape[1] // block
    each = tiles[0].shape[1] // block
    half = left_ref.shape[0] // 2
    tiles = list(tiles)
    n = 0
    while tiles:
        tile = tiles.pop(0)
        if tile.shape[0] == half:
            product = transposed_dot(left_ref[:half], tile[...])
            product = product + transposed_dot(left_ref[half:], tiles.pop(0)[...])
        else:
            product = transposed_dot(left_ref[...], tile[...])
        for t in range(each):
            for a in range(local):
                products_ref[(n * each + t) * local + a] = product[
                    a * block : (a + 1) * block, t * block : (t + 1) * block
                ]
        n += 1


def dense_kernel(block, tiles, blank, per_step, table_ref, left_ref, *refs):
    pieces = refs[:tiles]
    base_ref, out_hbm, products_ref, *held = refs[tiles:]
    out_ref = held[0] if held else out_hbm
    last = products_ref.shape[0] - 1
    if blank:
        products_ref[last] = jnp.zeros_like(products_ref[last])
    products_of(left_ref, pieces, products_ref, block)

    def step(i, _):
        for u in range(per_step):
            s = i * per_step + u
            product = products_ref[jnp.minimum(table_ref[s], last)]
            out_ref[s] = (base_ref[s].astype(F32) - product).astype(BF16)
        if held:
            copy(i).start()
        return _

    def copy(i):
        part = pl.ds(i * per_step, per_step)
        return pltpu.make_async_copy(out_ref.at[part], out_hbm.at[part], held[1].at[i])

    steps = table_ref.shape[0] // per_step
    lax.fori_loop(0, steps, step, 0)
    for i in range(steps if held else 0):
        copy(i).wait()


def dense(table, left, pieces, count, blank, base, per_step=16):
    slots, block, _ = base.shape
    local = left.shape[1] // block
    each = pieces[0].shape[1] // block
    return call(
        functools.partial(dense_kernel, block, len(pieces), blank, per_step),
        "dense",
        24,
        5,
        out_shape=jax.ShapeDtypeStruct(base.shape, BF16),
        in_specs=[SMEM] + [VMEM] * (2 + len(pieces)),
        out_specs=HBM if blank else VMEM,
        scratch_shapes=[pltpu.VMEM((count * each * local + blank, block, block), F32)]
        + ([pltpu.VMEM(base.shape, BF16), pltpu.SemaphoreType.DMA((slots // per_step,))] if blank else []),
    )(table, left, *pieces, base)


def last_kernel(block, tiles, first, table_ref, count_ref, left_ref, *refs):
    pieces = refs[:tiles]
    base_ref, _, out_hbm = refs[tiles : tiles + 3]
    products_ref, held_ref, sem = refs[tiles + 3 :]
    slots = table_ref.shape[0]
    products_of(left_ref, pieces, products_ref, block)

    def update(i, _):
        code = table_ref[i]
        s = code % slots
        product = products_ref[code // slots - first]
        held_ref[s] = (base_ref[s].astype(F32) - product).astype(BF16)
        pltpu.make_async_copy(held_ref.at[s], out_hbm.at[s], sem).start()
        return _

    def finish(i, _):
        pltpu.make_async_copy(held_ref.at[0], out_hbm.at[0], sem).wait()
        return _

    lax.fori_loop(0, count_ref[0], update, 0)
    lax.fori_loop(0, count_ref[0], finish, 0)


def last(table, count, left, pieces, base, done):
    slots, block, _ = base.shape
    local = left.shape[1] // block
    each = pieces[0].shape[1] // block
    rank = lax.axis_size("row") - 1
    return call(
        functools.partial(last_kernel, block, len(pieces), rank * each * local),
        "last",
        12,
        3,
        out_shape=jax.ShapeDtypeStruct(base.shape, BF16),
        in_specs=[SMEM] * 2 + [VMEM] * (2 + len(pieces)) + [HBM],
        out_specs=HBM,
        input_output_aliases={4 + len(pieces): 0},
        scratch_shapes=[
            pltpu.VMEM((each * local, block, block), F32),
            pltpu.VMEM((slots, block, block), BF16),
            pltpu.SemaphoreType.DMA,
        ],
    )(table, count, left, *pieces, base, done)


def per_device(
    panel_one,
    panel_two,
    inverse_one,
    inverse_two,
    column_blocks,
    row_map,
    targets,
    rows_one,
    cols_one,
    rows_two,
    cols_two,
):
    block = targets.shape[-1]
    slots = targets.shape[2]
    local = panel_one.shape[1] // block
    base = targets.reshape(slots, block, block)
    steps = lax.axis_size("row") // 2

    def ring(tile, between={}):
        half = tile.shape[0] // 2
        f = b = tile
        arrived = [tile]
        for k in range(1, steps + 1):
            if k == steps:
                f, b = f[:half], b[half:]
            f, b = ring_step(f, b)
            if between.get(k):
                earlier = between[k](arrived)
                f, b = after(f, *earlier), after(b, *earlier)
            arrived += [f, b]
        return arrived

    far_one = far_pieces(panel_one)
    raw = bridge_columns(panel_one, column_blocks, block)
    inverse_one_here = staged(inverse_one)
    own_one_here = staged(panel_one)
    masks = [1 << i for i in range(lax.axis_size("row").bit_length() - 1)][::-1]
    for mask in masks:
        other = xor_permute(raw, "row", mask)
        if mask == masks[0]:
            pieces_one = near_pieces(far_one)
            lower_one, own_one, tile_one = factor_one(
                inverse_one_here, [own_one_here] + pieces_one[1:], block
            )
            ring_one = ring(tile_one)
            other = after(other, tile_one)
        if mask == masks[-1]:
            far_two = far_pieces(after(panel_two, raw))
            inverse_two_here = staged(after(inverse_two, raw))
            own_two_here = staged(after(panel_two, raw))
            first = after(rows_one, raw).reshape(-1), cols_one.reshape(-1)
            second = after(rows_two, raw).reshape(-1), cols_two.reshape(-1)
            slots_one = slot_products(*first, local)
            slots_two = slot_products(*second, local)
            late, late_count = late_slots(
                slots_two, (lax.axis_size("row") - 1) * (local // lax.axis_size("col")) * local
            )
            row_map = after(row_map, raw) % local
            tables = (slots_one, slots_two, late, late_count, row_map)
            other = after(other, inverse_two_here, own_two_here, *tables, *ring_one[1:3])
        raw = raw + other
    base = staged(base)
    pieces_two = [own_two_here] + near_pieces(far_two)[1:]

    far_raw = far_pieces(raw)
    far_raw = {m: after(p, base) for m, p in far_raw.items()}
    tile, bridge = tile_two(
        row_map,
        inverse_one_here,
        inverse_two_here,
        lower_one,
        near_pieces(far_raw),
        pieces_two,
        block,
    )
    tile = after(tile, *ring_one[3:5])
    lower_two, own_two = factor_two(row_map, inverse_two_here, lower_one, bridge, pieces_two, block)
    part = dense(slots_one, lower_one, ring_one, 2 * steps, 0, base)
    result = []

    def most(arrived):
        result.append(dense(slots_two, lower_two, arrived, 2 * steps - 1, 1, part))
        return result

    ring_two = ring(tile, {1: lambda _: (own_two,) + tuple(ring_one[7:]), steps - 1: lambda _: (part,), steps: most})
    done = last(late, late_count, lower_two, ring_two[-2:], part, result[0])
    return own_one, own_two, done.reshape(targets.shape)


def solution(mesh):
    return jax.shard_map(
        per_device,
        mesh=mesh,
        in_specs=(
            P("col", "row"),
            P("col", "row"),
            P(),
            P(),
            P(),
            P("row"),
            P("row", "col", None, None, None),
            P("row", "col", None),
            P("row", "col", None),
            P("row", "col", None),
            P("row", "col", None),
        ),
        out_specs=(P("col", "row"), P("col", "row"), P("row", "col", None, None, None)),
        check_vma=False,
    )
```

```python
import functools

import jax
import jax.numpy as jnp
from jax import lax
from jax.experimental import pallas as pl
from jax.experimental.pallas import tpu as pltpu
from jax.sharding import PartitionSpec as P

VMEM = pl.BlockSpec(memory_space=pltpu.VMEM)
SMEM = pl.BlockSpec(memory_space=pltpu.SMEM)
HBM = pl.BlockSpec(memory_space=pltpu.HBM)
ANY = pl.BlockSpec(memory_space=pl.ANY)
F32 = jnp.float32
BF16 = jnp.bfloat16
TN = (((0,), (0,)), ((), ()))


def call(kernel, name, mib, micros, **kwargs):
    return pl.pallas_call(
        kernel,
        compiler_params=pltpu.CompilerParams(vmem_limit_bytes=mib and mib << 20),
        cost_estimate=pl.CostEstimate(
            flops=0, bytes_accessed=int(micros * 1e6), transcendentals=0
        ),
        name=name,
        **kwargs,
    )


def after(value, *earlier):
    return lax.optimization_barrier((value,) + earlier)[0]


def xor_permute(value, axis, mask):
    return lax.ppermute(value, axis, [(i, i ^ mask) for i in range(lax.axis_size(axis))])


def far_pieces(value):
    pieces = {0: value}
    bit = lax.axis_size("col") // 2
    while bit > 1:
        for m in list(pieces):
            pieces[m | bit] = xor_permute(pieces[m], "col", bit)
        bit //= 2
    return pieces


def near_pieces(pieces):
    pieces = dict(pieces)
    for m in list(pieces):
        pieces[m ^ 1] = xor_permute(pieces[m], "col", 1)
    return [pieces[m] for m in range(len(pieces))]


def ring_order(count):
    return list(range(0, count, 2)) + list(range(count - 1, 0, -2))


def ring_step(forward, backward):
    count = lax.axis_size("row")
    order = ring_order(count)
    ahead = [(order[i], order[(i + 1) % count]) for i in range(count)]
    back = [(b, a) for a, b in ahead]
    return lax.ppermute(forward, "row", ahead), lax.ppermute(backward, "row", back)


def arrival_rank(row):
    count = lax.axis_size("row")
    position = lambda r: jnp.where(r % 2 == 0, r // 2, count - 1 - r // 2)
    distance = (position(lax.axis_index("row")) - position(row)) % count
    ahead = jnp.maximum(2 * distance - 1, 0)
    return jnp.where(distance <= count // 2, ahead, 2 * (count - distance))


def slot_products(rows, cols, local):
    each = local // lax.axis_size("col")
    tile = cols % local // lax.axis_size("col")
    return (arrival_rank(cols // local) * each + tile) * local + rows % local


def late_slots(products, first):
    slots = products.shape[0]
    places = jnp.arange(slots, dtype=jnp.int32)
    late = products >= first
    place = jnp.sum(late[None, :] & (places[None, :] < places[:, None]), -1, dtype=jnp.int32)
    code = products * slots + places
    here = late[None, :] & (place[None, :] == places[:, None])
    table = jnp.sum(jnp.where(here, code[None, :], 0), -1, dtype=jnp.int32)
    return table, jnp.sum(late, dtype=jnp.int32).reshape(1)


def staged(value):
    return value * lax.optimization_barrier(jnp.ones((), value.dtype))


def bridge_kernel(block, local, blocks_ref, panel_ref, out_ref):
    row = lax.axis_index("row")
    for k in range(blocks_ref.shape[0]):
        piece = panel_ref[:, column(blocks_ref[k] % local, block)]
        keep = jnp.where(blocks_ref[k] // local == row, 1.0, 0.0).astype(BF16)
        out_ref[:, k * block : (k + 1) * block] = piece * keep


def bridge_columns(panel, column_blocks, block):
    slab = panel.shape[0]
    count = column_blocks.shape[0]
    return call(
        functools.partial(bridge_kernel, block, panel.shape[1] // block),
        "bridge_columns",
        8,
        1.3,
        out_shape=jax.ShapeDtypeStruct((slab, count * block), BF16),
        in_specs=[SMEM, VMEM],
        out_specs=VMEM,
    )(column_blocks, panel)


def slab_place(m, slab):
    start = pl.multiple_of((lax.axis_index("col") ^ m) * slab, slab)
    return pl.ds(start, slab)


def transposed_dot(left, right):
    return lax.dot_general(left, right, TN, preferred_element_type=F32)


def multiply(left_ref, right_ref, out_ref, step=256):
    for n in range(0, right_ref.shape[1], step):
        out_ref[:, n : n + step] = jnp.dot(
            left_ref[...], right_ref[:, n : n + step], preferred_element_type=F32
        ).astype(out_ref.dtype)


def column(j, block):
    return pl.ds(pl.multiple_of(j * block, block), block)


def own_blocks(block, width):
    for t in range(width // block):
        j = t * lax.axis_size("col") + lax.axis_index("col")
        yield slice(t * block, (t + 1) * block), j


def factor_one_kernel(block, count, *refs):
    inverse_ref, *pieces = refs[: 1 + count]
    lower_ref, own_ref, tile_ref, full_ref = refs[1 + count :]
    slab = own_ref.shape[0]
    for m, piece in enumerate(pieces):
        full_ref[slab_place(m, slab), :] = piece[...]
    multiply(inverse_ref, full_ref, lower_ref)
    own_ref[...] = lower_ref[slab_place(0, slab), :]
    for part, j in own_blocks(block, tile_ref.shape[1]):
        tile_ref[:, part] = lower_ref[:, column(j, block)]


def factor_one(inverse, pieces, block):
    width = inverse.shape[0]
    slab, columns = pieces[0].shape
    count = len(pieces)
    return call(
        functools.partial(factor_one_kernel, block, count),
        "factor_one",
        12,
        1.6,
        out_shape=(
            jax.ShapeDtypeStruct((width, columns), BF16),
            jax.ShapeDtypeStruct((slab, columns), BF16),
            jax.ShapeDtypeStruct((width, columns // count), BF16),
        ),
        in_specs=[VMEM] * (1 + count),
        out_specs=(VMEM,) * 3,
        scratch_shapes=[pltpu.VMEM((width, columns), BF16)],
    )(inverse, *pieces)


def tile_two_kernel(block, count, *refs):
    map_ref, one_ref, two_ref, lower_one_ref = refs[:4]
    raw = refs[4 : 4 + count]
    pieces = refs[4 + count : 4 + 2 * count]
    tile_ref, bridge_ref, raw_ref, full_ref, mapped_ref = refs[4 + 2 * count :]
    slab = raw[0].shape[0]
    for m, piece in enumerate(raw):
        raw_ref[slab_place(m, slab), :] = piece[...]
    multiply(one_ref, raw_ref, bridge_ref)
    for part, j in own_blocks(block, tile_ref.shape[1]):
        for m, piece in enumerate(pieces):
            full_ref[slab_place(m, slab), part] = piece[:, column(j, block)]
        mapped_ref[:, part] = lower_one_ref[:, column(map_ref[j], block)]
    update = transposed_dot(bridge_ref[...], mapped_ref[...])
    mapped_ref[...] = (full_ref[...].astype(F32) - update).astype(BF16)
    multiply(two_ref, mapped_ref, tile_ref)


def tile_two(row_map, inverse_one, inverse_two, lower_one, raw, pieces, block):
    width = inverse_one.shape[0]
    columns = pieces[0].shape[1]
    count = len(pieces)
    tile = columns // count
    return call(
        functools.partial(tile_two_kernel, block, count),
        "tile_two",
        12,
        1.6,
        out_shape=(
            jax.ShapeDtypeStruct((width, tile), BF16),
            jax.ShapeDtypeStruct((width, raw[0].shape[1]), BF16),
        ),
        in_specs=[SMEM] + [VMEM] * (3 + 2 * count),
        out_specs=(VMEM,) * 2,
        scratch_shapes=[
            pltpu.VMEM((width, raw[0].shape[1]), BF16),
            pltpu.VMEM((width, tile), BF16),
            pltpu.VMEM((width, tile), BF16),
        ],
    )(row_map, inverse_one, inverse_two, lower_one, *raw, *pieces)


def factor_two_kernel(block, count, *refs):
    map_ref, two_ref, lower_one_ref, bridge_ref, *pieces = refs[: 4 + count]
    lower_ref, own_ref, full_ref, mapped_ref = refs[4 + count :]
    slab = own_ref.shape[0]
    for m, piece in enumerate(pieces):
        full_ref[slab_place(m, slab), :] = piece[...]
    for j in range(map_ref.shape[0]):
        mapped_ref[:, j * block : (j + 1) * block] = lower_one_ref[:, column(map_ref[j], block)]
    step = 256
    for n in range(0, full_ref.shape[1], step):
        part = slice(n, n + step)
        update = transposed_dot(bridge_ref[...], mapped_ref[:, part])
        mapped_ref[:, part] = (full_ref[:, part].astype(F32) - update).astype(BF16)
    multiply(two_ref, mapped_ref, lower_ref)
    own_ref[...] = lower_ref[slab_place(0, slab), :]


def factor_two(row_map, inverse_two, lower_one, bridge, pieces, block):
    width = inverse_two.shape[0]
    slab, columns = pieces[0].shape
    count = len(pieces)
    return call(
        functools.partial(factor_two_kernel, block, count),
        "factor_two",
        12,
        2.4,
        out_shape=(
            jax.ShapeDtypeStruct((width, columns), BF16),
            jax.ShapeDtypeStruct((slab, columns), BF16),
        ),
        in_specs=[SMEM] + [VMEM] * (3 + count),
        out_specs=(VMEM,) * 2,
        scratch_shapes=[pltpu.VMEM((width, columns), BF16), pltpu.VMEM((width, columns), BF16)],
    )(row_map, inverse_two, lower_one, bridge, *pieces)


def products_of(left_ref, tiles, products_ref, block):
    local = left_ref.shape[1] // block
    each = tiles[0].shape[1] // block
    half = left_ref.shape[0] // 2
    tiles = list(tiles)
    n = 0
    while tiles:
        tile = tiles.pop(0)
        if tile.shape[0] == half:
            product = transposed_dot(left_ref[:half], tile[...])
            product = product + transposed_dot(left_ref[half:], tiles.pop(0)[...])
        else:
            product = transposed_dot(left_ref[...], tile[...])
        for t in range(each):
            for a in range(local):
                products_ref[(n * each + t) * local + a] = product[
                    a * block : (a + 1) * block, t * block : (t + 1) * block
                ]
        n += 1


def dense_kernel(block, tiles, blank, per_step, table_ref, left_ref, *refs):
    pieces = refs[:tiles]
    base_ref, out_hbm, products_ref, *held = refs[tiles:]
    out_ref = held[0] if held else out_hbm
    last = products_ref.shape[0] - 1
    if blank:
        products_ref[last] = jnp.zeros_like(products_ref[last])
    products_of(left_ref, pieces, products_ref, block)

    def step(i, _):
        for u in range(per_step):
            s = i * per_step + u
            product = products_ref[jnp.minimum(table_ref[s], last)]
            out_ref[s] = (base_ref[s].astype(F32) - product).astype(BF16)
        if held:
            copy(i).start()
        return _

    def copy(i):
        part = pl.ds(i * per_step, per_step)
        return pltpu.make_async_copy(out_ref.at[part], out_hbm.at[part], held[1].at[i])

    steps = table_ref.shape[0] // per_step
    lax.fori_loop(0, steps, step, 0)
    for i in range(steps if held else 0):
        copy(i).wait()


def dense(table, left, pieces, count, blank, base, per_step=16):
    slots, block, _ = base.shape
    local = left.shape[1] // block
    each = pieces[0].shape[1] // block
    return call(
        functools.partial(dense_kernel, block, len(pieces), blank, per_step),
        "dense",
        24,
        5,
        out_shape=jax.ShapeDtypeStruct(base.shape, BF16),
        in_specs=[SMEM] + [VMEM] * (2 + len(pieces)),
        out_specs=HBM if blank else VMEM,
        scratch_shapes=[pltpu.VMEM((count * each * local + blank, block, block), F32)]
        + ([pltpu.VMEM(base.shape, BF16), pltpu.SemaphoreType.DMA((slots // per_step,))] if blank else []),
    )(table, left, *pieces, base)


def last_kernel(block, tiles, first, table_ref, count_ref, left_ref, *refs):
    pieces = refs[:tiles]
    base_ref, _, out_hbm = refs[tiles : tiles + 3]
    products_ref, held_ref, sem = refs[tiles + 3 :]
    slots = table_ref.shape[0]
    products_of(left_ref, pieces, products_ref, block)

    def update(i, _):
        code = table_ref[i]
        s = code % slots
        product = products_ref[code // slots - first]
        held_ref[s] = (base_ref[s].astype(F32) - product).astype(BF16)
        pltpu.make_async_copy(held_ref.at[s], out_hbm.at[s], sem).start()
        return _

    def finish(i, _):
        pltpu.make_async_copy(held_ref.at[0], out_hbm.at[0], sem).wait()
        return _

    lax.fori_loop(0, count_ref[0], update, 0)
    lax.fori_loop(0, count_ref[0], finish, 0)


def last(table, count, left, pieces, base, done):
    slots, block, _ = base.shape
    local = left.shape[1] // block
    each = pieces[0].shape[1] // block
    rank = lax.axis_size("row") - 1
    return call(
        functools.partial(last_kernel, block, len(pieces), rank * each * local),
        "last",
        12,
        3,
        out_shape=jax.ShapeDtypeStruct(base.shape, BF16),
        in_specs=[SMEM] * 2 + [VMEM] * (2 + len(pieces)) + [HBM],
        out_specs=HBM,
        input_output_aliases={4 + len(pieces): 0},
        scratch_shapes=[
            pltpu.VMEM((each * local, block, block), F32),
            pltpu.VMEM((slots, block, block), BF16),
            pltpu.SemaphoreType.DMA,
        ],
    )(table, count, left, *pieces, base, done)


def per_device(
    panel_one,
    panel_two,
    inverse_one,
    inverse_two,
    column_blocks,
    row_map,
    targets,
    rows_one,
    cols_one,
    rows_two,
    cols_two,
):
    block = targets.shape[-1]
    slots = targets.shape[2]
    local = panel_one.shape[1] // block
    base = targets.reshape(slots, block, block)
    steps = lax.axis_size("row") // 2

    def go_on(arrived, *earlier):
        k = (len(arrived) + 1) // 2
        f, b = arrived[-2:] if k > 1 else arrived * 2
        if earlier:
            f, b = after(f, *earlier), after(b, *earlier)
        if k == steps:
            half = f.shape[0] // 2
            f, b = f[:half], b[half:]
        arrived += ring_step(f, b)

    def meet(arrived, *earlier):
        arrived[-2:] = [after(piece, *earlier) for piece in arrived[-2:]]

    raw = bridge_columns(panel_one, column_blocks, block)
    far_one = far_pieces(after(panel_one, raw))
    inverse_one_here = staged(inverse_one)
    own_one_here = staged(panel_one)
    masks = [1 << i for i in range(lax.axis_size("row").bit_length() - 1)][::-1]
    for at, mask in enumerate(masks):
        other = xor_permute(raw, "row", mask)
        if at == 0:
            other = after(other, inverse_one_here, own_one_here)
        if at == 1:
            far_one = {m: after(p, raw) for m, p in far_one.items()}
            pieces_one = near_pieces(far_one)
            lower_one, own_one, tile_one = factor_one(
                inverse_one_here, [own_one_here] + pieces_one[1:], block
            )
            ring_one = [tile_one]
            go_on(ring_one)
            other = after(other, tile_one)
        if at == 2:
            far_two = far_pieces(after(panel_two, raw))
            inverse_two_here = staged(after(inverse_two, raw))
            own_two_here = staged(after(panel_two, raw))
            other = after(other, inverse_two_here, own_two_here)
            first = after(rows_one, raw).reshape(-1), cols_one.reshape(-1)
            second = after(rows_two, raw).reshape(-1), cols_two.reshape(-1)
            slots_one = slot_products(*first, local)
            slots_two = slot_products(*second, local)
            late, late_count = late_slots(
                slots_two, (lax.axis_size("row") - 1) * (local // lax.axis_size("col")) * local
            )
            row_map = after(row_map, raw) % local
            other = after(other, slots_one, slots_two, late, late_count, row_map)
        raw = raw + other
    base = staged(base)
    go_on(ring_one)
    pieces_two = [own_two_here] + near_pieces(far_two)[1:]
    far_raw = far_pieces(raw)
    far_raw = {m: after(p, *ring_one[1:3]) for m, p in far_raw.items()}
    tile, bridge = tile_two(
        row_map, inverse_one_here, inverse_two_here, lower_one, near_pieces(far_raw), pieces_two, block
    )
    ring_two = [tile]
    go_on(ring_two)
    lower_two, own_two = factor_two(row_map, inverse_two_here, lower_one, bridge, pieces_two, block)
    while len(ring_one) < 2 * steps + 1:
        go_on(ring_one)
    part = dense(slots_one, lower_one, ring_one, 2 * steps, 0, base)
    meet(ring_two, own_two, *ring_one[3:5], *ring_one[7:])
    for k in range(2, steps):
        go_on(ring_two)
        if k == steps - 1:
            meet(ring_two, part)
    go_on(ring_two)
    done = dense(slots_two, lower_two, ring_two[:-2], 2 * steps - 1, 1, part)
    meet(ring_two, done)
    done = last(late, late_count, lower_two, ring_two[-2:], part, done)
    return own_one, own_two, done.reshape(targets.shape)


def solution(mesh):
    return jax.shard_map(
        per_device,
        mesh=mesh,
        in_specs=(
            P("col", "row"),
            P("col", "row"),
            P(),
            P(),
            P(),
            P("row"),
            P("row", "col", None, None, None),
            P("row", "col", None),
            P("row", "col", None),
            P("row", "col", None),
            P("row", "col", None),
        ),
        out_specs=(P("col", "row"), P("col", "row"), P("row", "col", None, None, None)),
        check_vma=False,
    )
```

```python
import functools

import jax
import jax.numpy as jnp
from jax import lax
from jax.experimental import pallas as pl
from jax.experimental.pallas import tpu as pltpu
from jax.sharding import PartitionSpec as P

VMEM = pl.BlockSpec(memory_space=pltpu.VMEM)
SMEM = pl.BlockSpec(memory_space=pltpu.SMEM)
HBM = pl.BlockSpec(memory_space=pltpu.HBM)
ANY = pl.BlockSpec(memory_space=pl.ANY)
F32 = jnp.float32
BF16 = jnp.bfloat16
TN = (((0,), (0,)), ((), ()))


def call(kernel, name, mib, micros, **kwargs):
    return pl.pallas_call(
        kernel,
        compiler_params=pltpu.CompilerParams(vmem_limit_bytes=mib and mib << 20),
        cost_estimate=pl.CostEstimate(
            flops=0, bytes_accessed=int(micros * 1e6), transcendentals=0
        ),
        name=name,
        **kwargs,
    )


def after(value, *earlier):
    return lax.optimization_barrier((value,) + earlier)[0]


def xor_permute(value, axis, mask):
    return lax.ppermute(value, axis, [(i, i ^ mask) for i in range(lax.axis_size(axis))])


def far_pieces(value):
    pieces = {0: value}
    bit = lax.axis_size("col") // 2
    while bit > 1:
        for m in list(pieces):
            pieces[m | bit] = xor_permute(pieces[m], "col", bit)
        bit //= 2
    return pieces


def near_pieces(pieces):
    pieces = dict(pieces)
    for m in list(pieces):
        pieces[m ^ 1] = xor_permute(pieces[m], "col", 1)
    return [pieces[m] for m in range(len(pieces))]


def ring_order(count):
    return list(range(0, count, 2)) + list(range(count - 1, 0, -2))


def ring_step(forward, backward):
    count = lax.axis_size("row")
    order = ring_order(count)
    ahead = [(order[i], order[(i + 1) % count]) for i in range(count)]
    back = [(b, a) for a, b in ahead]
    return lax.ppermute(forward, "row", ahead), lax.ppermute(backward, "row", back)


def arrival_rank(row):
    count = lax.axis_size("row")
    position = lambda r: jnp.where(r % 2 == 0, r // 2, count - 1 - r // 2)
    distance = (position(lax.axis_index("row")) - position(row)) % count
    ahead = jnp.maximum(2 * distance - 1, 0)
    return jnp.where(distance <= count // 2, ahead, 2 * (count - distance))


def slot_products(rows, cols, local):
    each = local // lax.axis_size("col")
    tile = cols % local // lax.axis_size("col")
    return (arrival_rank(cols // local) * each + tile) * local + rows % local


def late_slots(products, first):
    slots = products.shape[0]
    places = jnp.arange(slots, dtype=jnp.int32)
    late = products >= first
    place = jnp.sum(late[None, :] & (places[None, :] < places[:, None]), -1, dtype=jnp.int32)
    here = late[None, :] & (place[None, :] == places[:, None])
    listed = lambda values: jnp.sum(jnp.where(here, values[None, :], 0), -1, dtype=jnp.int32)
    return listed(places), listed(products - first), jnp.sum(late, dtype=jnp.int32).reshape(1)


def within(products, first, count):
    place = products - first
    return jnp.where((place >= 0) & (place < count), place, count)


def staged(value):
    return value * lax.optimization_barrier(jnp.ones((), value.dtype))


def bridge_kernel(block, local, blocks_ref, panel_ref, out_ref):
    row = lax.axis_index("row")
    for k in range(blocks_ref.shape[0]):
        piece = panel_ref[:, column(blocks_ref[k] % local, block)]
        keep = jnp.where(blocks_ref[k] // local == row, 1.0, 0.0).astype(BF16)
        out_ref[:, k * block : (k + 1) * block] = piece * keep


def bridge_columns(panel, column_blocks, block):
    slab = panel.shape[0]
    count = column_blocks.shape[0]
    return call(
        functools.partial(bridge_kernel, block, panel.shape[1] // block),
        "bridge_columns",
        8,
        1.3,
        out_shape=jax.ShapeDtypeStruct((slab, count * block), BF16),
        in_specs=[SMEM, VMEM],
        out_specs=VMEM,
    )(column_blocks, panel)


def slab_place(m, slab):
    start = pl.multiple_of((lax.axis_index("col") ^ m) * slab, slab)
    return pl.ds(start, slab)


def transposed_dot(left, right):
    return lax.dot_general(left, right, TN, preferred_element_type=F32)


def multiply(left_ref, right_ref, out_ref, step=256):
    for n in range(0, right_ref.shape[1], step):
        out_ref[:, n : n + step] = jnp.dot(
            left_ref[...], right_ref[:, n : n + step], preferred_element_type=F32
        ).astype(out_ref.dtype)


def column(j, block):
    return pl.ds(pl.multiple_of(j * block, block), block)


def own_blocks(block, width):
    for t in range(width // block):
        j = t * lax.axis_size("col") + lax.axis_index("col")
        yield slice(t * block, (t + 1) * block), j


def factor_one_kernel(block, count, *refs):
    inverse_ref, *pieces = refs[: 1 + count]
    lower_ref, own_ref, tile_ref, full_ref = refs[1 + count :]
    slab = own_ref.shape[0]
    for m, piece in enumerate(pieces):
        full_ref[slab_place(m, slab), :] = piece[...]
    multiply(inverse_ref, full_ref, lower_ref)
    own_ref[...] = lower_ref[slab_place(0, slab), :]
    for part, j in own_blocks(block, tile_ref.shape[1]):
        tile_ref[:, part] = lower_ref[:, column(j, block)]


def factor_one(inverse, pieces, block):
    width = inverse.shape[0]
    slab, columns = pieces[0].shape
    count = len(pieces)
    return call(
        functools.partial(factor_one_kernel, block, count),
        "factor_one",
        12,
        1.6,
        out_shape=(
            jax.ShapeDtypeStruct((width, columns), BF16),
            jax.ShapeDtypeStruct((slab, columns), BF16),
            jax.ShapeDtypeStruct((width, columns // count), BF16),
        ),
        in_specs=[VMEM] * (1 + count),
        out_specs=(VMEM,) * 3,
        scratch_shapes=[pltpu.VMEM((width, columns), BF16)],
    )(inverse, *pieces)


def tile_two_kernel(block, count, *refs):
    map_ref, one_ref, two_ref, lower_one_ref = refs[:4]
    raw = refs[4 : 4 + count]
    pieces = refs[4 + count : 4 + 2 * count]
    tile_ref, bridge_ref, raw_ref, full_ref, mapped_ref = refs[4 + 2 * count :]
    slab = raw[0].shape[0]
    for m, piece in enumerate(raw):
        raw_ref[slab_place(m, slab), :] = piece[...]
    multiply(one_ref, raw_ref, bridge_ref)
    for part, j in own_blocks(block, tile_ref.shape[1]):
        for m, piece in enumerate(pieces):
            full_ref[slab_place(m, slab), part] = piece[:, column(j, block)]
        mapped_ref[:, part] = lower_one_ref[:, column(map_ref[j], block)]
    update = transposed_dot(bridge_ref[...], mapped_ref[...])
    mapped_ref[...] = (full_ref[...].astype(F32) - update).astype(BF16)
    multiply(two_ref, mapped_ref, tile_ref)


def tile_two(row_map, inverse_one, inverse_two, lower_one, raw, pieces, block):
    width = inverse_one.shape[0]
    columns = pieces[0].shape[1]
    count = len(pieces)
    tile = columns // count
    return call(
        functools.partial(tile_two_kernel, block, count),
        "tile_two",
        12,
        1.6,
        out_shape=(
            jax.ShapeDtypeStruct((width, tile), BF16),
            jax.ShapeDtypeStruct((width, raw[0].shape[1]), BF16),
        ),
        in_specs=[SMEM] + [VMEM] * (3 + 2 * count),
        out_specs=(VMEM,) * 2,
        scratch_shapes=[
            pltpu.VMEM((width, raw[0].shape[1]), BF16),
            pltpu.VMEM((width, tile), BF16),
            pltpu.VMEM((width, tile), BF16),
        ],
    )(row_map, inverse_one, inverse_two, lower_one, *raw, *pieces)


def factor_two_kernel(block, count, *refs):
    map_ref, two_ref, lower_one_ref, bridge_ref, *pieces = refs[: 4 + count]
    lower_ref, own_ref, full_ref, mapped_ref = refs[4 + count :]
    slab = own_ref.shape[0]
    for m, piece in enumerate(pieces):
        full_ref[slab_place(m, slab), :] = piece[...]
    for j in range(map_ref.shape[0]):
        mapped_ref[:, j * block : (j + 1) * block] = lower_one_ref[:, column(map_ref[j], block)]
    step = 256
    for n in range(0, full_ref.shape[1], step):
        part = slice(n, n + step)
        update = transposed_dot(bridge_ref[...], mapped_ref[:, part])
        mapped_ref[:, part] = (full_ref[:, part].astype(F32) - update).astype(BF16)
    multiply(two_ref, mapped_ref, lower_ref)
    own_ref[...] = lower_ref[slab_place(0, slab), :]


def factor_two(row_map, inverse_two, lower_one, bridge, pieces, block):
    width = inverse_two.shape[0]
    slab, columns = pieces[0].shape
    count = len(pieces)
    return call(
        functools.partial(factor_two_kernel, block, count),
        "factor_two",
        12,
        2.4,
        out_shape=(
            jax.ShapeDtypeStruct((width, columns), BF16),
            jax.ShapeDtypeStruct((slab, columns), BF16),
        ),
        in_specs=[SMEM] + [VMEM] * (3 + count),
        out_specs=(VMEM,) * 2,
        scratch_shapes=[pltpu.VMEM((width, columns), BF16), pltpu.VMEM((width, columns), BF16)],
    )(row_map, inverse_two, lower_one, bridge, *pieces)


def products_of(left_ref, tiles, products_ref, block):
    local = left_ref.shape[1] // block
    each = tiles[0].shape[1] // block
    half = left_ref.shape[0] // 2
    tiles = list(tiles)
    n = 0
    while tiles:
        tile = tiles.pop(0)
        if tile.shape[0] == half:
            product = transposed_dot(left_ref[:half], tile[...])
            product = product + transposed_dot(left_ref[half:], tiles.pop(0)[...])
        else:
            product = transposed_dot(left_ref[...], tile[...])
        for t in range(each):
            for a in range(local):
                products_ref[(n * each + t) * local + a] = product[
                    a * block : (a + 1) * block, t * block : (t + 1) * block
                ]
        n += 1


def dense_kernel(block, groups, per_step, *refs):
    tables, refs = refs[: len(groups)], refs[len(groups) :]
    lefts, pieces = [], []
    for tiles in groups:
        lefts, pieces, refs = lefts + [refs[0]], pieces + [refs[1 : 1 + tiles]], refs[1 + tiles :]
    base_ref, out_hbm, *products = refs[: 2 + len(groups)]
    held = refs[2 + len(groups) :]
    out_ref = held[0] if held else out_hbm
    for left_ref, tiles, products_ref in zip(lefts, pieces, products):
        last = products_ref.shape[0] - 1
        products_ref[last] = jnp.zeros_like(products_ref[last])
        products_of(left_ref, tiles, products_ref, block)

    def copy(i):
        part = pl.ds(i * per_step, per_step)
        return pltpu.make_async_copy(out_ref.at[part], out_hbm.at[part], held[1].at[i])

    def step(i, _):
        for u in range(per_step):
            s = i * per_step + u
            value = base_ref[s].astype(F32)
            for table_ref, products_ref in zip(tables, products):
                value = value - products_ref[table_ref[s]]
            out_ref[s] = value.astype(BF16)
        if held:
            copy(i).start()
        return _

    steps = tables[0].shape[0] // per_step
    lax.fori_loop(0, steps, step, 0)
    for i in range(steps if held else 0):
        copy(i).wait()


def dense(groups, base, final, per_step=16):
    slots, block, _ = base.shape
    products = []
    for _, left, pieces in groups:
        rows = left.shape[1] // block * (pieces[0].shape[1] // block)
        tiles = sum(p.shape[0] for p in pieces) // left.shape[0]
        products.append(pltpu.VMEM((tiles * rows + 1, block, block), F32))
    held = [pltpu.VMEM(base.shape, BF16), pltpu.SemaphoreType.DMA((slots // per_step,))]
    operands = [x for _, left, pieces in groups for x in (left, *pieces)]
    return call(
        functools.partial(dense_kernel, block, [len(p) for _, _, p in groups], per_step),
        "dense",
        24,
        5,
        out_shape=jax.ShapeDtypeStruct(base.shape, BF16),
        in_specs=[SMEM] * len(groups) + [VMEM] * (1 + len(operands)),
        out_specs=HBM if final else VMEM,
        scratch_shapes=products + (held if final else []),
    )(*[table for table, _, _ in groups], *operands, base)


def last_kernel(block, tiles, slots_ref, places_ref, count_ref, left_ref, *refs):
    pieces = refs[:tiles]
    base_ref, _, out_hbm = refs[tiles : tiles + 3]
    products_ref, held_ref, sem = refs[tiles + 3 :]
    count = count_ref[0]
    products_of(left_ref, pieces, products_ref, block)

    def update(i, _):
        s = slots_ref[i]
        product = products_ref[places_ref[i]]
        held_ref[s] = (base_ref[s].astype(F32) - product).astype(BF16)
        pltpu.make_async_copy(held_ref.at[s], out_hbm.at[s], sem).start()
        return _

    def finish(size, i, _):
        part = pl.ds(0, size)
        pltpu.make_async_copy(held_ref.at[part], out_hbm.at[part], sem).wait()
        return _

    lax.fori_loop(0, count, update, 0)
    lax.fori_loop(0, count // 8, functools.partial(finish, 8), 0)
    lax.fori_loop(0, count % 8, functools.partial(finish, 1), 0)


def last(late, left, pieces, base, done):
    slots, block, _ = base.shape
    local = left.shape[1] // block
    each = pieces[0].shape[1] // block
    return call(
        functools.partial(last_kernel, block, len(pieces)),
        "last",
        12,
        3,
        out_shape=jax.ShapeDtypeStruct(base.shape, BF16),
        in_specs=[SMEM] * 3 + [VMEM] * (2 + len(pieces)) + [HBM],
        out_specs=HBM,
        input_output_aliases={5 + len(pieces): 0},
        scratch_shapes=[
            pltpu.VMEM((each * local, block, block), F32),
            pltpu.VMEM((slots, block, block), BF16),
            pltpu.SemaphoreType.DMA,
        ],
    )(*late, left, *pieces, base, done)


def per_device(
    panel_one,
    panel_two,
    inverse_one,
    inverse_two,
    column_blocks,
    row_map,
    targets,
    rows_one,
    cols_one,
    rows_two,
    cols_two,
):
    block = targets.shape[-1]
    slots = targets.shape[2]
    local = panel_one.shape[1] // block
    base = targets.reshape(slots, block, block)
    steps = lax.axis_size("row") // 2

    def go_on(arrived, *earlier):
        k = (len(arrived) + 1) // 2
        f, b = arrived[-2:] if k > 1 else arrived * 2
        if earlier:
            f, b = after(f, *earlier), after(b, *earlier)
        if k == steps:
            half = f.shape[0] // 2
            f, b = f[:half], b[half:]
        arrived += ring_step(f, b)

    def meet(arrived, *earlier):
        arrived[-2:] = [after(piece, *earlier) for piece in arrived[-2:]]

    far_one = far_pieces(panel_one)
    raw = bridge_columns(panel_one, column_blocks, block)
    inverse_one_here = staged(inverse_one)
    own_one_here = staged(panel_one)
    masks = [1 << i for i in range(lax.axis_size("row").bit_length() - 1)][::-1]
    for at, mask in enumerate(masks):
        other = xor_permute(raw, "row", mask)
        if at == 0:
            pieces_one = near_pieces(far_one)
            lower_one, own_one, tile_one = factor_one(
                inverse_one_here, [own_one_here] + pieces_one[1:], block
            )
            ring_one = [tile_one]
            go_on(ring_one)
            other = after(other, tile_one)
        if at == 2:
            far_two = far_pieces(after(panel_two, raw))
            inverse_two_here = staged(after(inverse_two, raw))
            own_two_here = staged(after(panel_two, raw))
            other = after(other, inverse_two_here, own_two_here)
            first = after(rows_one, raw).reshape(-1), cols_one.reshape(-1)
            second = after(rows_two, raw).reshape(-1), cols_two.reshape(-1)
            slots_one = slot_products(*first, local)
            slots_two = slot_products(*second, local)
            tile_products = local // lax.axis_size("col") * local
            late = late_slots(slots_two, (2 * steps - 1) * tile_products)
            early = within(slots_two, 0, 3 * tile_products)
            middle = within(slots_two, 3 * tile_products, (2 * steps - 1 - 3) * tile_products)
            row_map = after(row_map, raw) % local
            other = after(other, slots_one, early, middle, *late, row_map)
            other = after(other, *ring_one[1:3])
        raw = raw + other
    base = staged(base)
    go_on(ring_one)
    pieces_two = [own_two_here] + near_pieces(far_two)[1:]
    far_raw = far_pieces(raw)
    far_raw = {m: after(p, base) for m, p in far_raw.items()}
    tile, bridge = tile_two(
        row_map, inverse_one_here, inverse_two_here, lower_one, near_pieces(far_raw), pieces_two, block
    )
    tile = after(tile, *ring_one[3:5])
    ring_two = [tile]
    go_on(ring_two)
    lower_two, own_two = factor_two(row_map, inverse_two_here, lower_one, bridge, pieces_two, block)
    while len(ring_one) < 2 * steps + 1:
        go_on(ring_one)
    meet(ring_two, own_two, *ring_one[3:5], *ring_one[7:])
    part = dense(
        [(slots_one, lower_one, ring_one), (early, lower_two, ring_two[:3])], base, final=False
    )
    for k in range(2, steps):
        go_on(ring_two)
        if k == 2:
            meet(ring_two, part)
    go_on(ring_two)
    done = dense([(middle, lower_two, ring_two[3:-2])], part, final=True)
    meet(ring_two, done)
    done = last(late, lower_two, ring_two[-2:], part, done)
    return own_one, own_two, done.reshape(targets.shape)


def solution(mesh):
    return jax.shard_map(
        per_device,
        mesh=mesh,
        in_specs=(
            P("col", "row"),
            P("col", "row"),
            P(),
            P(),
            P(),
            P("row"),
            P("row", "col", None, None, None),
            P("row", "col", None),
            P("row", "col", None),
            P("row", "col", None),
            P("row", "col", None),
        ),
        out_specs=(P("col", "row"), P("col", "row"), P("row", "col", None, None, None)),
        check_vma=False,
    )
```

```python
import functools

import jax
import jax.numpy as jnp
from jax import lax
from jax.experimental import pallas as pl
from jax.experimental.pallas import tpu as pltpu
from jax.sharding import PartitionSpec as P

VMEM = pl.BlockSpec(memory_space=pltpu.VMEM)
SMEM = pl.BlockSpec(memory_space=pltpu.SMEM)
HBM = pl.BlockSpec(memory_space=pltpu.HBM)
ANY = pl.BlockSpec(memory_space=pl.ANY)
F32 = jnp.float32
BF16 = jnp.bfloat16
TN = (((0,), (0,)), ((), ()))


def call(kernel, name, mib, micros, **kwargs):
    return pl.pallas_call(
        kernel,
        compiler_params=pltpu.CompilerParams(vmem_limit_bytes=mib and mib << 20),
        cost_estimate=pl.CostEstimate(
            flops=0, bytes_accessed=int(micros * 1e6), transcendentals=0
        ),
        name=name,
        **kwargs,
    )


def after(value, *earlier):
    return lax.optimization_barrier((value,) + earlier)[0]


def xor_permute(value, axis, mask):
    return lax.ppermute(value, axis, [(i, i ^ mask) for i in range(lax.axis_size(axis))])


def far_pieces(value):
    pieces = {0: value}
    bit = lax.axis_size("col") // 2
    while bit > 1:
        for m in list(pieces):
            pieces[m | bit] = xor_permute(pieces[m], "col", bit)
        bit //= 2
    return pieces


def near_pieces(pieces):
    pieces = dict(pieces)
    for m in list(pieces):
        pieces[m ^ 1] = xor_permute(pieces[m], "col", 1)
    return [pieces[m] for m in range(len(pieces))]


def ring_order(count):
    return list(range(0, count, 2)) + list(range(count - 1, 0, -2))


def ring_step(forward, backward):
    count = lax.axis_size("row")
    order = ring_order(count)
    ahead = [(order[i], order[(i + 1) % count]) for i in range(count)]
    back = [(b, a) for a, b in ahead]
    return lax.ppermute(forward, "row", ahead), lax.ppermute(backward, "row", back)


def arrival_rank(row):
    count = lax.axis_size("row")
    position = lambda r: jnp.where(r % 2 == 0, r // 2, count - 1 - r // 2)
    distance = (position(lax.axis_index("row")) - position(row)) % count
    ahead = jnp.maximum(2 * distance - 1, 0)
    return jnp.where(distance <= count // 2, ahead, 2 * (count - distance))


def slot_products(rows, cols, local):
    each = local // lax.axis_size("col")
    tile = cols % local // lax.axis_size("col")
    return (arrival_rank(cols // local) * each + tile) * local + rows % local


def late_slots(products, first):
    slots = products.shape[0]
    places = jnp.arange(slots, dtype=jnp.int32)
    late = products >= first
    place = jnp.sum(late[None, :] & (places[None, :] < places[:, None]), -1, dtype=jnp.int32)
    here = late[None, :] & (place[None, :] == places[:, None])
    listed = lambda values: jnp.sum(jnp.where(here, values[None, :], 0), -1, dtype=jnp.int32)
    return listed(places), listed(products - first), jnp.sum(late, dtype=jnp.int32).reshape(1)


def within(products, first, count):
    place = products - first
    return jnp.where((place >= 0) & (place < count), place, count)


def staged(value):
    return value * lax.optimization_barrier(jnp.ones((), value.dtype))


def bridge_kernel(block, local, blocks_ref, panel_ref, out_ref):
    row = lax.axis_index("row")
    for k in range(blocks_ref.shape[0]):
        piece = panel_ref[:, column(blocks_ref[k] % local, block)]
        keep = jnp.where(blocks_ref[k] // local == row, 1.0, 0.0).astype(BF16)
        out_ref[:, k * block : (k + 1) * block] = piece * keep


def bridge_columns(panel, column_blocks, block):
    slab = panel.shape[0]
    count = column_blocks.shape[0]
    return call(
        functools.partial(bridge_kernel, block, panel.shape[1] // block),
        "bridge_columns",
        8,
        1.3,
        out_shape=jax.ShapeDtypeStruct((slab, count * block), BF16),
        in_specs=[SMEM, VMEM],
        out_specs=VMEM,
    )(column_blocks, panel)


def slab_place(m, slab):
    start = pl.multiple_of((lax.axis_index("col") ^ m) * slab, slab)
    return pl.ds(start, slab)


def transposed_dot(left, right):
    return lax.dot_general(left, right, TN, preferred_element_type=F32)


def multiply(left_ref, right_ref, out_ref, step=256):
    for n in range(0, right_ref.shape[1], step):
        out_ref[:, n : n + step] = jnp.dot(
            left_ref[...], right_ref[:, n : n + step], preferred_element_type=F32
        ).astype(out_ref.dtype)


def column(j, block):
    return pl.ds(pl.multiple_of(j * block, block), block)


def own_blocks(block, width):
    for t in range(width // block):
        j = t * lax.axis_size("col") + lax.axis_index("col")
        yield slice(t * block, (t + 1) * block), j


def factor_one_kernel(block, count, *refs):
    inverse_ref, *pieces = refs[: 1 + count]
    lower_ref, own_ref, tile_ref, full_ref = refs[1 + count :]
    slab = own_ref.shape[0]
    for m, piece in enumerate(pieces):
        full_ref[slab_place(m, slab), :] = piece[...]
    multiply(inverse_ref, full_ref, lower_ref)
    own_ref[...] = lower_ref[slab_place(0, slab), :]
    for part, j in own_blocks(block, tile_ref.shape[1]):
        tile_ref[:, part] = lower_ref[:, column(j, block)]


def factor_one(inverse, pieces, block):
    width = inverse.shape[0]
    slab, columns = pieces[0].shape
    count = len(pieces)
    return call(
        functools.partial(factor_one_kernel, block, count),
        "factor_one",
        12,
        1.6,
        out_shape=(
            jax.ShapeDtypeStruct((width, columns), BF16),
            jax.ShapeDtypeStruct((slab, columns), BF16),
            jax.ShapeDtypeStruct((width, columns // count), BF16),
        ),
        in_specs=[VMEM] * (1 + count),
        out_specs=(VMEM,) * 3,
        scratch_shapes=[pltpu.VMEM((width, columns), BF16)],
    )(inverse, *pieces)


def tile_two_kernel(block, count, *refs):
    map_ref, one_ref, two_ref, lower_one_ref = refs[:4]
    raw = refs[4 : 4 + count]
    pieces = refs[4 + count : 4 + 2 * count]
    tile_ref, bridge_ref, raw_ref, full_ref, mapped_ref = refs[4 + 2 * count :]
    slab = raw[0].shape[0]
    for m, piece in enumerate(raw):
        raw_ref[slab_place(m, slab), :] = piece[...]
    multiply(one_ref, raw_ref, bridge_ref)
    for part, j in own_blocks(block, tile_ref.shape[1]):
        for m, piece in enumerate(pieces):
            full_ref[slab_place(m, slab), part] = piece[:, column(j, block)]
        mapped_ref[:, part] = lower_one_ref[:, column(map_ref[j], block)]
    update = transposed_dot(bridge_ref[...], mapped_ref[...])
    mapped_ref[...] = (full_ref[...].astype(F32) - update).astype(BF16)
    multiply(two_ref, mapped_ref, tile_ref)


def tile_two(row_map, inverse_one, inverse_two, lower_one, raw, pieces, block):
    width = inverse_one.shape[0]
    columns = pieces[0].shape[1]
    count = len(pieces)
    tile = columns // count
    return call(
        functools.partial(tile_two_kernel, block, count),
        "tile_two",
        12,
        1.6,
        out_shape=(
            jax.ShapeDtypeStruct((width, tile), BF16),
            jax.ShapeDtypeStruct((width, raw[0].shape[1]), BF16),
        ),
        in_specs=[SMEM] + [VMEM] * (3 + 2 * count),
        out_specs=(VMEM,) * 2,
        scratch_shapes=[
            pltpu.VMEM((width, raw[0].shape[1]), BF16),
            pltpu.VMEM((width, tile), BF16),
            pltpu.VMEM((width, tile), BF16),
        ],
    )(row_map, inverse_one, inverse_two, lower_one, *raw, *pieces)


def factor_two_kernel(block, count, *refs):
    map_ref, two_ref, lower_one_ref, bridge_ref, *pieces = refs[: 4 + count]
    lower_ref, own_ref, full_ref, mapped_ref = refs[4 + count :]
    slab = own_ref.shape[0]
    for m, piece in enumerate(pieces):
        full_ref[slab_place(m, slab), :] = piece[...]
    for j in range(map_ref.shape[0]):
        mapped_ref[:, j * block : (j + 1) * block] = lower_one_ref[:, column(map_ref[j], block)]
    step = 256
    for n in range(0, full_ref.shape[1], step):
        part = slice(n, n + step)
        update = transposed_dot(bridge_ref[...], mapped_ref[:, part])
        mapped_ref[:, part] = (full_ref[:, part].astype(F32) - update).astype(BF16)
    multiply(two_ref, mapped_ref, lower_ref)
    own_ref[...] = lower_ref[slab_place(0, slab), :]


def factor_two(row_map, inverse_two, lower_one, bridge, pieces, block):
    width = inverse_two.shape[0]
    slab, columns = pieces[0].shape
    count = len(pieces)
    return call(
        functools.partial(factor_two_kernel, block, count),
        "factor_two",
        12,
        2.4,
        out_shape=(
            jax.ShapeDtypeStruct((width, columns), BF16),
            jax.ShapeDtypeStruct((slab, columns), BF16),
        ),
        in_specs=[SMEM] + [VMEM] * (3 + count),
        out_specs=(VMEM,) * 2,
        scratch_shapes=[pltpu.VMEM((width, columns), BF16), pltpu.VMEM((width, columns), BF16)],
    )(row_map, inverse_two, lower_one, bridge, *pieces)


def products_of(left_ref, tiles, products_ref, block):
    local = left_ref.shape[1] // block
    each = tiles[0].shape[1] // block
    half = left_ref.shape[0] // 2
    tiles = list(tiles)
    n = 0
    while tiles:
        tile = tiles.pop(0)
        if tile.shape[0] == half:
            product = transposed_dot(left_ref[:half], tile[...])
            product = product + transposed_dot(left_ref[half:], tiles.pop(0)[...])
        else:
            product = transposed_dot(left_ref[...], tile[...])
        for t in range(each):
            for a in range(local):
                products_ref[(n * each + t) * local + a] = product[
                    a * block : (a + 1) * block, t * block : (t + 1) * block
                ]
        n += 1


def dense_kernel(block, groups, per_step, *refs):
    tables, refs = refs[: len(groups)], refs[len(groups) :]
    lefts, pieces = [], []
    for tiles in groups:
        lefts, pieces, refs = lefts + [refs[0]], pieces + [refs[1 : 1 + tiles]], refs[1 + tiles :]
    base_ref, out_hbm, *products = refs[: 2 + len(groups)]
    held = refs[2 + len(groups) :]
    out_ref = held[0] if held else out_hbm
    for left_ref, tiles, products_ref in zip(lefts, pieces, products):
        last = products_ref.shape[0] - 1
        products_ref[last] = jnp.zeros_like(products_ref[last])
        products_of(left_ref, tiles, products_ref, block)

    def copy(i):
        part = pl.ds(i * per_step, per_step)
        return pltpu.make_async_copy(out_ref.at[part], out_hbm.at[part], held[1].at[i])

    def step(i, _):
        for u in range(per_step):
            s = i * per_step + u
            value = base_ref[s].astype(F32)
            for table_ref, products_ref in zip(tables, products):
                value = value - products_ref[table_ref[s]]
            out_ref[s] = value.astype(BF16)
        if held:
            copy(i).start()
        return _

    steps = tables[0].shape[0] // per_step
    lax.fori_loop(0, steps, step, 0)
    for i in range(steps if held else 0):
        copy(i).wait()


def dense(groups, base, final, per_step=16):
    slots, block, _ = base.shape
    products = []
    for _, left, pieces in groups:
        rows = left.shape[1] // block * (pieces[0].shape[1] // block)
        tiles = sum(p.shape[0] for p in pieces) // left.shape[0]
        products.append(pltpu.VMEM((tiles * rows + 1, block, block), F32))
    held = [pltpu.VMEM(base.shape, BF16), pltpu.SemaphoreType.DMA((slots // per_step,))]
    operands = [x for _, left, pieces in groups for x in (left, *pieces)]
    return call(
        functools.partial(dense_kernel, block, [len(p) for _, _, p in groups], per_step),
        "dense",
        24,
        5,
        out_shape=jax.ShapeDtypeStruct(base.shape, BF16),
        in_specs=[SMEM] * len(groups) + [VMEM] * (1 + len(operands)),
        out_specs=HBM if final else VMEM,
        scratch_shapes=products + (held if final else []),
    )(*[table for table, _, _ in groups], *operands, base)


def last_kernel(block, tiles, slots_ref, places_ref, count_ref, left_ref, *refs):
    pieces = refs[:tiles]
    base_ref, _, out_hbm = refs[tiles : tiles + 3]
    products_ref, held_ref, sem = refs[tiles + 3 :]
    count = count_ref[0]
    products_of(left_ref, pieces, products_ref, block)

    def update(i, _):
        s = slots_ref[i]
        product = products_ref[places_ref[i]]
        held_ref[s] = (base_ref[s].astype(F32) - product).astype(BF16)
        pltpu.make_async_copy(held_ref.at[s], out_hbm.at[s], sem).start()
        return _

    def finish(size, i, _):
        part = pl.ds(0, size)
        pltpu.make_async_copy(held_ref.at[part], out_hbm.at[part], sem).wait()
        return _

    lax.fori_loop(0, count, update, 0)
    lax.fori_loop(0, count // 8, functools.partial(finish, 8), 0)
    lax.fori_loop(0, count % 8, functools.partial(finish, 1), 0)


def last(late, left, pieces, base, done):
    slots, block, _ = base.shape
    local = left.shape[1] // block
    each = pieces[0].shape[1] // block
    return call(
        functools.partial(last_kernel, block, len(pieces)),
        "last",
        12,
        3,
        out_shape=jax.ShapeDtypeStruct(base.shape, BF16),
        in_specs=[SMEM] * 3 + [VMEM] * (2 + len(pieces)) + [HBM],
        out_specs=HBM,
        input_output_aliases={5 + len(pieces): 0},
        scratch_shapes=[
            pltpu.VMEM((each * local, block, block), F32),
            pltpu.VMEM((slots, block, block), BF16),
            pltpu.SemaphoreType.DMA,
        ],
    )(*late, left, *pieces, base, done)


def per_device(
    panel_one,
    panel_two,
    inverse_one,
    inverse_two,
    column_blocks,
    row_map,
    targets,
    rows_one,
    cols_one,
    rows_two,
    cols_two,
):
    block = targets.shape[-1]
    slots = targets.shape[2]
    local = panel_one.shape[1] // block
    base = targets.reshape(slots, block, block)
    steps = lax.axis_size("row") // 2

    def go_on(arrived, *earlier):
        k = (len(arrived) + 1) // 2
        f, b = arrived[-2:] if k > 1 else arrived * 2
        if earlier:
            f, b = after(f, *earlier), after(b, *earlier)
        if k == steps:
            half = f.shape[0] // 2
            f, b = f[:half], b[half:]
        arrived += ring_step(f, b)

    def meet(arrived, *earlier):
        arrived[-2:] = [after(piece, *earlier) for piece in arrived[-2:]]

    far_one = far_pieces(panel_one)
    raw = bridge_columns(panel_one, column_blocks, block)
    inverse_one_here = staged(inverse_one)
    own_one_here = staged(panel_one)
    masks = [1 << i for i in range(lax.axis_size("row").bit_length() - 1)][::-1]
    for at, mask in enumerate(masks):
        other = xor_permute(raw, "row", mask)
        if at == 0:
            pieces_one = near_pieces(far_one)
            lower_one, own_one, tile_one = factor_one(
                inverse_one_here, [own_one_here] + pieces_one[1:], block
            )
            ring_one = [tile_one]
            go_on(ring_one)
            other = after(other, tile_one)
        if at == 1:
            far_two = far_pieces(after(panel_two, raw))
        if at == 2:
            inverse_two_here = staged(after(inverse_two, raw))
            own_two_here = staged(after(panel_two, raw))
            other = after(other, inverse_two_here, own_two_here)
            first = after(rows_one, raw).reshape(-1), cols_one.reshape(-1)
            second = after(rows_two, raw).reshape(-1), cols_two.reshape(-1)
            slots_one = slot_products(*first, local)
            slots_two = slot_products(*second, local)
            tile_products = local // lax.axis_size("col") * local
            late = late_slots(slots_two, (2 * steps - 1) * tile_products)
            early = within(slots_two, 0, 3 * tile_products)
            middle = within(slots_two, 3 * tile_products, (2 * steps - 1 - 3) * tile_products)
            row_map = after(row_map, raw) % local
            other = after(other, slots_one, early, middle, *late, row_map)
            other = after(other, *ring_one[1:3])
        raw = raw + other
    base = staged(base)
    go_on(ring_one)
    pieces_two = [own_two_here] + near_pieces(far_two)[1:]
    far_raw = far_pieces(raw)
    far_raw = {m: after(p, base) for m, p in far_raw.items()}
    raw = near_pieces(far_raw)
    tile, bridge = tile_two(
        row_map, inverse_one_here, inverse_two_here, lower_one, raw, pieces_two, block
    )
    tile = after(tile, *ring_one[3:5])
    ring_two = [tile]
    go_on(ring_two)
    lower_two, own_two = factor_two(row_map, inverse_two_here, lower_one, bridge, pieces_two, block)
    while len(ring_one) < 2 * steps + 1:
        go_on(ring_one)
    meet(ring_two, own_two, *ring_one[3:5], *ring_one[7:])
    part = dense(
        [(slots_one, lower_one, ring_one), (early, lower_two, ring_two[:3])], base, final=False
    )
    for k in range(2, steps):
        go_on(ring_two)
        if k == 2:
            meet(ring_two, part)
    go_on(ring_two)
    done = dense([(middle, lower_two, ring_two[3:-2])], part, final=True)
    meet(ring_two, done)
    done = last(late, lower_two, ring_two[-2:], part, done)
    return own_one, own_two, done.reshape(targets.shape)


def solution(mesh):
    return jax.shard_map(
        per_device,
        mesh=mesh,
        in_specs=(
            P("col", "row"),
            P("col", "row"),
            P(),
            P(),
            P(),
            P("row"),
            P("row", "col", None, None, None),
            P("row", "col", None),
            P("row", "col", None),
            P("row", "col", None),
            P("row", "col", None),
        ),
        out_specs=(P("col", "row"), P("col", "row"), P("row", "col", None, None, None)),
        check_vma=False,
    )
```

```python
import functools

import jax
import jax.numpy as jnp
from jax import lax
from jax.experimental import pallas as pl
from jax.experimental.pallas import tpu as pltpu
from jax.sharding import PartitionSpec as P

VMEM = pl.BlockSpec(memory_space=pltpu.VMEM)
SMEM = pl.BlockSpec(memory_space=pltpu.SMEM)
HBM = pl.BlockSpec(memory_space=pltpu.HBM)
ANY = pl.BlockSpec(memory_space=pl.ANY)
F32 = jnp.float32
BF16 = jnp.bfloat16
TN = (((0,), (0,)), ((), ()))


def call(kernel, name, mib, micros, **kwargs):
    return pl.pallas_call(
        kernel,
        compiler_params=pltpu.CompilerParams(vmem_limit_bytes=mib and mib << 20),
        cost_estimate=pl.CostEstimate(
            flops=0, bytes_accessed=int(micros * 1e6), transcendentals=0
        ),
        name=name,
        **kwargs,
    )


def after(value, *earlier):
    return lax.optimization_barrier((value,) + earlier)[0]


def xor_permute(value, axis, mask):
    return lax.ppermute(value, axis, [(i, i ^ mask) for i in range(lax.axis_size(axis))])


def far_pieces(value):
    pieces = {0: value}
    bit = lax.axis_size("col") // 2
    while bit > 1:
        for m in list(pieces):
            pieces[m | bit] = xor_permute(pieces[m], "col", bit)
        bit //= 2
    return pieces


def near_pieces(pieces):
    pieces = dict(pieces)
    for m in list(pieces):
        pieces[m ^ 1] = xor_permute(pieces[m], "col", 1)
    return [pieces[m] for m in range(len(pieces))]


def ring_order(count):
    return list(range(0, count, 2)) + list(range(count - 1, 0, -2))


def ring_step(forward, backward):
    count = lax.axis_size("row")
    order = ring_order(count)
    ahead = [(order[i], order[(i + 1) % count]) for i in range(count)]
    back = [(b, a) for a, b in ahead]
    return lax.ppermute(forward, "row", ahead), lax.ppermute(backward, "row", back)


def arrival_rank(row):
    count = lax.axis_size("row")
    position = lambda r: jnp.where(r % 2 == 0, r // 2, count - 1 - r // 2)
    distance = (position(lax.axis_index("row")) - position(row)) % count
    ahead = jnp.maximum(2 * distance - 1, 0)
    return jnp.where(distance <= count // 2, ahead, 2 * (count - distance))


def slot_products(rows, cols, local):
    each = local // lax.axis_size("col")
    tile = cols % local // lax.axis_size("col")
    return (arrival_rank(cols // local) * each + tile) * local + rows % local


def late_slots(products, first):
    slots = products.shape[0]
    places = jnp.arange(slots, dtype=jnp.int32)
    late = products >= first
    place = jnp.sum(late[None, :] & (places[None, :] < places[:, None]), -1, dtype=jnp.int32)
    here = late[None, :] & (place[None, :] == places[:, None])
    listed = lambda values: jnp.sum(jnp.where(here, values[None, :], 0), -1, dtype=jnp.int32)
    return listed(places), listed(products - first), jnp.sum(late, dtype=jnp.int32).reshape(1)


def within(products, first, count):
    place = products - first
    return jnp.where((place >= 0) & (place < count), place, count)


def staged(value):
    return value * lax.optimization_barrier(jnp.ones((), value.dtype))


def bridge_kernel(block, local, blocks_ref, panel_ref, out_ref):
    row = lax.axis_index("row")
    for k in range(blocks_ref.shape[0]):
        piece = panel_ref[:, column(blocks_ref[k] % local, block)]
        keep = jnp.where(blocks_ref[k] // local == row, 1.0, 0.0).astype(BF16)
        out_ref[:, k * block : (k + 1) * block] = piece * keep


def bridge_columns(panel, column_blocks, block):
    slab = panel.shape[0]
    count = column_blocks.shape[0]
    return call(
        functools.partial(bridge_kernel, block, panel.shape[1] // block),
        "bridge_columns",
        8,
        1.3,
        out_shape=jax.ShapeDtypeStruct((slab, count * block), BF16),
        in_specs=[SMEM, VMEM],
        out_specs=VMEM,
    )(column_blocks, panel)


def slab_place(m, slab):
    start = pl.multiple_of((lax.axis_index("col") ^ m) * slab, slab)
    return pl.ds(start, slab)


def transposed_dot(left, right):
    return lax.dot_general(left, right, TN, preferred_element_type=F32)


def multiply(left_ref, right_ref, out_ref, step=256):
    for n in range(0, right_ref.shape[1], step):
        out_ref[:, n : n + step] = jnp.dot(
            left_ref[...], right_ref[:, n : n + step], preferred_element_type=F32
        ).astype(out_ref.dtype)


def column(j, block):
    return pl.ds(pl.multiple_of(j * block, block), block)


def own_blocks(block, width):
    for t in range(width // block):
        j = t * lax.axis_size("col") + lax.axis_index("col")
        yield slice(t * block, (t + 1) * block), j


def factor_one_kernel(block, count, *refs):
    inverse_ref, *pieces = refs[: 1 + count]
    lower_ref, own_ref, tile_ref, full_ref = refs[1 + count :]
    slab = own_ref.shape[0]
    for m, piece in enumerate(pieces):
        full_ref[slab_place(m, slab), :] = piece[...]
    multiply(inverse_ref, full_ref, lower_ref)
    own_ref[...] = lower_ref[slab_place(0, slab), :]
    for part, j in own_blocks(block, tile_ref.shape[1]):
        tile_ref[:, part] = lower_ref[:, column(j, block)]


def factor_one(inverse, pieces, block):
    width = inverse.shape[0]
    slab, columns = pieces[0].shape
    count = len(pieces)
    return call(
        functools.partial(factor_one_kernel, block, count),
        "factor_one",
        12,
        1.6,
        out_shape=(
            jax.ShapeDtypeStruct((width, columns), BF16),
            jax.ShapeDtypeStruct((slab, columns), BF16),
            jax.ShapeDtypeStruct((width, columns // count), BF16),
        ),
        in_specs=[VMEM] * (1 + count),
        out_specs=(VMEM,) * 3,
        scratch_shapes=[pltpu.VMEM((width, columns), BF16)],
    )(inverse, *pieces)


def tile_two_kernel(block, count, *refs):
    map_ref, one_ref, two_ref, lower_one_ref = refs[:4]
    raw = refs[4 : 4 + count]
    pieces = refs[4 + count : 4 + 2 * count]
    tile_ref, bridge_ref, raw_ref, full_ref, mapped_ref = refs[4 + 2 * count :]
    slab = raw[0].shape[0]
    for m, piece in enumerate(raw):
        raw_ref[slab_place(m, slab), :] = piece[...]
    multiply(one_ref, raw_ref, bridge_ref)
    for part, j in own_blocks(block, tile_ref.shape[1]):
        for m, piece in enumerate(pieces):
            full_ref[slab_place(m, slab), part] = piece[:, column(j, block)]
        mapped_ref[:, part] = lower_one_ref[:, column(map_ref[j], block)]
    update = transposed_dot(bridge_ref[...], mapped_ref[...])
    mapped_ref[...] = (full_ref[...].astype(F32) - update).astype(BF16)
    multiply(two_ref, mapped_ref, tile_ref)


def tile_two(row_map, inverse_one, inverse_two, lower_one, raw, pieces, block):
    width = inverse_one.shape[0]
    columns = pieces[0].shape[1]
    count = len(pieces)
    tile = columns // count
    return call(
        functools.partial(tile_two_kernel, block, count),
        "tile_two",
        12,
        1.6,
        out_shape=(
            jax.ShapeDtypeStruct((width, tile), BF16),
            jax.ShapeDtypeStruct((width, raw[0].shape[1]), BF16),
        ),
        in_specs=[SMEM] + [VMEM] * (3 + 2 * count),
        out_specs=(VMEM,) * 2,
        scratch_shapes=[
            pltpu.VMEM((width, raw[0].shape[1]), BF16),
            pltpu.VMEM((width, tile), BF16),
            pltpu.VMEM((width, tile), BF16),
        ],
    )(row_map, inverse_one, inverse_two, lower_one, *raw, *pieces)


def factor_two_kernel(block, count, *refs):
    map_ref, two_ref, lower_one_ref, bridge_ref, *pieces = refs[: 4 + count]
    lower_ref, own_ref, full_ref, mapped_ref = refs[4 + count :]
    slab = own_ref.shape[0]
    for m, piece in enumerate(pieces):
        full_ref[slab_place(m, slab), :] = piece[...]
    for j in range(map_ref.shape[0]):
        mapped_ref[:, j * block : (j + 1) * block] = lower_one_ref[:, column(map_ref[j], block)]
    step = 256
    for n in range(0, full_ref.shape[1], step):
        part = slice(n, n + step)
        update = transposed_dot(bridge_ref[...], mapped_ref[:, part])
        mapped_ref[:, part] = (full_ref[:, part].astype(F32) - update).astype(BF16)
    multiply(two_ref, mapped_ref, lower_ref)
    own_ref[...] = lower_ref[slab_place(0, slab), :]


def factor_two(row_map, inverse_two, lower_one, bridge, pieces, block):
    width = inverse_two.shape[0]
    slab, columns = pieces[0].shape
    count = len(pieces)
    return call(
        functools.partial(factor_two_kernel, block, count),
        "factor_two",
        12,
        2.4,
        out_shape=(
            jax.ShapeDtypeStruct((width, columns), BF16),
            jax.ShapeDtypeStruct((slab, columns), BF16),
        ),
        in_specs=[SMEM] + [VMEM] * (3 + count),
        out_specs=(VMEM,) * 2,
        scratch_shapes=[pltpu.VMEM((width, columns), BF16), pltpu.VMEM((width, columns), BF16)],
    )(row_map, inverse_two, lower_one, bridge, *pieces)


def products_of(left_ref, tiles, products_ref, block):
    local = left_ref.shape[1] // block
    each = tiles[0].shape[1] // block
    half = left_ref.shape[0] // 2
    tiles = list(tiles)
    n = 0
    while tiles:
        tile = tiles.pop(0)
        if tile.shape[0] == half:
            rest = tiles.pop(0)
            for begin in range(0, left_ref.shape[1], 2 * block):
                rows = slice(begin, begin + 2 * block)
                product = transposed_dot(left_ref[:half, rows], tile[...])
                product = product + transposed_dot(left_ref[half:, rows], rest[...])
                for t in range(each):
                    for a in range(2):
                        products_ref[(n * each + t) * local + begin // block + a] = product[
                            a * block : (a + 1) * block, t * block : (t + 1) * block
                        ]
            n += 1
            continue
        else:
            product = transposed_dot(left_ref[...], tile[...])
        for t in range(each):
            for a in range(local):
                products_ref[(n * each + t) * local + a] = product[
                    a * block : (a + 1) * block, t * block : (t + 1) * block
                ]
        n += 1


def dense_kernel(block, groups, per_step, *refs):
    tables, refs = refs[: len(groups)], refs[len(groups) :]
    lefts, pieces = [], []
    for tiles in groups:
        lefts, pieces, refs = lefts + [refs[0]], pieces + [refs[1 : 1 + tiles]], refs[1 + tiles :]
    base_ref, out_hbm, *products = refs[: 2 + len(groups)]
    held = refs[2 + len(groups) :]
    out_ref = held[0] if held else out_hbm
    for left_ref, tiles, products_ref in zip(lefts, pieces, products):
        last = products_ref.shape[0] - 1
        products_ref[last] = jnp.zeros_like(products_ref[last])
        products_of(left_ref, tiles, products_ref, block)

    def copy(i):
        part = pl.ds(i * per_step, per_step)
        return pltpu.make_async_copy(out_ref.at[part], out_hbm.at[part], held[1].at[i])

    def step(i, _):
        for u in range(per_step):
            s = i * per_step + u
            value = base_ref[s].astype(F32)
            for table_ref, products_ref in zip(tables, products):
                value = value - products_ref[table_ref[s]]
            out_ref[s] = value.astype(BF16)
        if held:
            copy(i).start()
        return _

    steps = tables[0].shape[0] // per_step
    lax.fori_loop(0, steps, step, 0)
    for i in range(steps if held else 0):
        copy(i).wait()


def dense(groups, base, final, per_step=16):
    slots, block, _ = base.shape
    products = []
    for _, left, pieces in groups:
        rows = left.shape[1] // block * (pieces[0].shape[1] // block)
        tiles = sum(p.shape[0] for p in pieces) // left.shape[0]
        products.append(pltpu.VMEM((tiles * rows + 1, block, block), F32))
    held = [pltpu.VMEM(base.shape, BF16), pltpu.SemaphoreType.DMA((slots // per_step,))]
    operands = [x for _, left, pieces in groups for x in (left, *pieces)]
    return call(
        functools.partial(dense_kernel, block, [len(p) for _, _, p in groups], per_step),
        "dense",
        24,
        5,
        out_shape=jax.ShapeDtypeStruct(base.shape, BF16),
        in_specs=[SMEM] * len(groups) + [VMEM] * (1 + len(operands)),
        out_specs=HBM if final else VMEM,
        scratch_shapes=products + (held if final else []),
    )(*[table for table, _, _ in groups], *operands, base)


def last_kernel(block, tiles, slots_ref, places_ref, count_ref, left_ref, *refs):
    pieces = refs[:tiles]
    base_ref, _, out_hbm = refs[tiles : tiles + 3]
    products_ref, held_ref, sem = refs[tiles + 3 :]
    count = count_ref[0]
    products_of(left_ref, pieces, products_ref, block)

    def update(i, _):
        s = slots_ref[i]
        product = products_ref[places_ref[i]]
        held_ref[s] = (base_ref[s].astype(F32) - product).astype(BF16)
        pltpu.make_async_copy(held_ref.at[s], out_hbm.at[s], sem).start()
        return _

    def finish(size, i, _):
        part = pl.ds(0, size)
        pltpu.make_async_copy(held_ref.at[part], out_hbm.at[part], sem).wait()
        return _

    lax.fori_loop(0, count, update, 0)
    lax.fori_loop(0, count // 8, functools.partial(finish, 8), 0)
    lax.fori_loop(0, count % 8, functools.partial(finish, 1), 0)


def last(late, left, pieces, base, done):
    slots, block, _ = base.shape
    local = left.shape[1] // block
    each = pieces[0].shape[1] // block
    return call(
        functools.partial(last_kernel, block, len(pieces)),
        "last",
        12,
        3,
        out_shape=jax.ShapeDtypeStruct(base.shape, BF16),
        in_specs=[SMEM] * 3 + [VMEM] * (2 + len(pieces)) + [HBM],
        out_specs=HBM,
        input_output_aliases={5 + len(pieces): 0},
        scratch_shapes=[
            pltpu.VMEM((each * local, block, block), F32),
            pltpu.VMEM((slots, block, block), BF16),
            pltpu.SemaphoreType.DMA,
        ],
    )(*late, left, *pieces, base, done)


def per_device(
    panel_one,
    panel_two,
    inverse_one,
    inverse_two,
    column_blocks,
    row_map,
    targets,
    rows_one,
    cols_one,
    rows_two,
    cols_two,
):
    block = targets.shape[-1]
    slots = targets.shape[2]
    local = panel_one.shape[1] // block
    base = targets.reshape(slots, block, block)
    steps = lax.axis_size("row") // 2

    def go_on(arrived, *earlier):
        k = (len(arrived) + 1) // 2
        f, b = arrived[-2:] if k > 1 else arrived * 2
        if earlier:
            f, b = after(f, *earlier), after(b, *earlier)
        if k == steps:
            half = f.shape[0] // 2
            f, b = f[:half], b[half:]
        arrived += ring_step(f, b)

    def meet(arrived, *earlier):
        arrived[-2:] = [after(piece, *earlier) for piece in arrived[-2:]]

    far_one = far_pieces(panel_one)
    raw = bridge_columns(panel_one, column_blocks, block)
    inverse_one_here = staged(inverse_one)
    own_one_here = staged(panel_one)
    masks = [1 << i for i in range(lax.axis_size("row").bit_length() - 1)][::-1]
    for at, mask in enumerate(masks):
        other = xor_permute(raw, "row", mask)
        if at == 0:
            pieces_one = near_pieces(far_one)
            lower_one, own_one, tile_one = factor_one(
                inverse_one_here, [own_one_here] + pieces_one[1:], block
            )
            ring_one = [tile_one]
            go_on(ring_one)
            other = after(other, tile_one)
        if at == 1:
            far_two = far_pieces(after(panel_two, raw))
        if at == 2:
            inverse_two_here = staged(after(inverse_two, raw))
            own_two_here = staged(after(panel_two, raw))
            other = after(other, inverse_two_here, own_two_here)
            first = after(rows_one, raw).reshape(-1), cols_one.reshape(-1)
            second = after(rows_two, raw).reshape(-1), cols_two.reshape(-1)
            slots_one = slot_products(*first, local)
            slots_two = slot_products(*second, local)
            tile_products = local // lax.axis_size("col") * local
            late = late_slots(slots_two, (2 * steps - 1) * tile_products)
            early = within(slots_two, 0, 3 * tile_products)
            middle = within(slots_two, 3 * tile_products, (2 * steps - 1 - 3) * tile_products)
            row_map = after(row_map, raw) % local
            other = after(other, slots_one, early, middle, *late, row_map)
            other = after(other, *ring_one[1:3])
        raw = raw + other
    base = staged(base)
    go_on(ring_one)
    pieces_two = [own_two_here] + near_pieces(far_two)[1:]
    far_raw = far_pieces(raw)
    far_raw = {m: after(p, base) for m, p in far_raw.items()}
    raw = near_pieces(far_raw)
    tile, bridge = tile_two(
        row_map, inverse_one_here, inverse_two_here, lower_one, raw, pieces_two, block
    )
    tile = after(tile, *ring_one[3:5])
    ring_two = [tile]
    go_on(ring_two)
    lower_two, own_two = factor_two(row_map, inverse_two_here, lower_one, bridge, pieces_two, block)
    while len(ring_one) < 2 * steps + 1:
        go_on(ring_one)
    meet(ring_two, own_two, *ring_one[3:5], *ring_one[7:])
    part = dense(
        [(slots_one, lower_one, ring_one), (early, lower_two, ring_two[:3])], base, final=False
    )
    for k in range(2, steps):
        go_on(ring_two)
        if k == 2:
            meet(ring_two, part)
    go_on(ring_two)
    done = dense([(middle, lower_two, ring_two[3:-2])], part, final=True)
    meet(ring_two, done)
    done = last(late, lower_two, ring_two[-2:], part, done)
    return own_one, own_two, done.reshape(targets.shape)


def solution(mesh):
    return jax.shard_map(
        per_device,
        mesh=mesh,
        in_specs=(
            P("col", "row"),
            P("col", "row"),
            P(),
            P(),
            P(),
            P("row"),
            P("row", "col", None, None, None),
            P("row", "col", None),
            P("row", "col", None),
            P("row", "col", None),
            P("row", "col", None),
        ),
        out_specs=(P("col", "row"), P("col", "row"), P("row", "col", None, None, None)),
        check_vma=False,
    )
```
